32 devices in a mesh: groups: 2 (over x), modes: 16 (over z, y, core).
Axes of the slice: x: 2, y: 2, z: 4, core: 2. Of those that a mesh axis runs over, the one named last changes fastest.
Arguments:
- mode_fields: bfloat16 [256, 256, 2048], P(('groups', 'modes')), parts along dimension 0, may hold values from -0.59765625 to 0.59765625
- coeff: float32 [256], P('groups'), parts along dimension 0, may hold values from -6 to 6
- eigen: float32 [256], P('groups'), parts along dimension 0, may hold values from 0.1 to 100
- map_friction: float32 [512, 2048], P(('groups', 'modes')), parts along dimension 0, may hold values from 1 to 2.5
- bed: float32 [512, 2048], P(('groups', 'modes')), parts along dimension 0, may hold values from -5 to 5
- smb: float32 [512, 2048], P(('groups', 'modes')), parts along dimension 0, may hold values from -0.6 to 0.4
- thickness: float32 [512, 2048], P(('groups', 'modes')), parts along dimension 0, may hold values from 1.9 to 2.6
Outputs:
- log_friction: float32 [512, 2048], P(('groups', 'modes')), parts along dimension 0
- final_thickness: float32 [512, 2048], P(('groups', 'modes')), parts along dimension 0
The draws below stay inside these ranges and needn't reach their ends.
There are 2 independent parts, one for each index of `groups`. The reference program is written for one: setup_inputs(seed, part) draws one part's arguments, and reference() takes and returns one part's arrays. A program takes and returns all parts, laid end to end along the dimension named above; each array names one. Nothing has to cross between parts.
All inputs are finite; a program needn't handle non-finite values.
Results may differ from the reference program's by a relative error of at most 0.0014.
Values may be sent and summed in bfloat16 or wider, within the bound.
No kernel may reach another device: no remote copies, remote signals or barrier semaphores. Data moves between devices by JAX's collectives and lax.ppermute only.
A program may use at most 64 MiB of HBM per device.

```python
import math
import jax
import jax.numpy as jnp

MODES = 128
NY = 2048
STEPS = 8
NX = 256


def draw_bed(key, part):
    key_list = jax.random.split(jax.random.fold_in(key, 17), 2)
    phase_pair = jax.random.uniform(key_list[0], (2,), jnp.float32, 0.0, 2.0 * math.pi)
    row_index = jnp.arange(NX, dtype=jnp.float32)[:, None]
    column_index = jnp.arange(NY, dtype=jnp.float32)[None, :]
    wave_number = 2.0 * math.pi / 48.0
    amplitude = 2.0
    roughness = jnp.clip(0.25 * jax.random.normal(key_list[1], (NX, NY), jnp.float32), -0.75, 0.75)
    smooth_part = amplitude * (jnp.sin(wave_number * row_index + phase_pair[0]) + jnp.sin(wave_number * column_index + phase_pair[1]))
    return (smooth_part + roughness).astype(jnp.float32)


def with_spikes(drawn, stream_key, source, target, parts, factor):
    owner, partner = [(jnp.arange(drawn.shape[axis_at]) // (drawn.shape[axis_at] // parts)).reshape([-1 if axis == axis_at else 1 for axis in range(drawn.ndim)]) for axis_at in (source, target)]
    chosen = jax.random.permutation(stream_key, parts)[partner]
    strong = (owner == chosen) | (owner == (partner + parts // 2) % parts)
    return jnp.where(strong, factor * drawn, drawn)


def block_scale(own_key, extent, cuts, smallest, largest):
    level, own = 1.0, jax.random.fold_in(own_key, 6)
    for position, parts in cuts:
        heights = jnp.exp(jax.random.uniform(jax.random.fold_in(own, position), (parts,), jnp.float32, smallest / len(cuts), largest / len(cuts)))
        level = level * jnp.repeat(heights, extent[position] // parts).reshape([-1 if axis == position else 1 for axis in range(len(extent))])
    return level


def centred(stream_key, extent, width, most, cuts=(), kind=jnp.bfloat16):
    gain = block_scale(stream_key, extent, cuts, -0.22, 0.18) if cuts else 1.0
    drawn = jax.random.normal(stream_key, extent, jnp.float32) * width * gain
    return jnp.minimum(jnp.maximum(drawn, -most), most).astype(kind)


def bell_draw_with(stream_key, dims, deviation, reach, cuts, heavy, kind=jnp.bfloat16):
    drawn = deviation * jax.random.normal(stream_key, dims, jnp.float32)
    if cuts:
        drawn = drawn * block_scale(stream_key, dims, cuts, -0.22, 0.18)
    return jnp.clip(with_spikes(drawn, jax.random.fold_in(stream_key, 3), *heavy), -reach, reach).astype(kind)


def setup_inputs(seed: int = 0, part: int = 0) -> dict:
    streams_of = jax.random.split(jax.random.key(seed), 8)
    part_splits = jax.random.split(jax.random.fold_in(streams_of[7], part), 8)
    return {
        "mode_fields": bell_draw_with(part_splits[0], (MODES, NX, NY), 0.1, 0.59765625, ((0, 16),), (0, 1, 16, 2.0)),
        "coeff": centred(part_splits[1], (MODES,), 1.0, 6.0, (), jnp.float32),
        "eigen": jnp.clip(jnp.exp(jax.random.uniform(part_splits[2], (MODES,), jnp.float32, math.log(0.1), math.log(100.0))), 0.1, 100.0),
        "map_friction": jnp.clip(1.0 + 1.5 * jax.random.uniform(part_splits[3], (NX, NY), jnp.float32) ** block_scale(part_splits[3], (NX, NY), ((0, 16),), -0.2, 0.2), 1.0, 2.5),
        "bed": draw_bed(jax.random.fold_in(jax.random.fold_in(streams_of[7], part), 71), part),
        "smb": jnp.clip(-0.6 + 1 * jax.random.uniform(part_splits[5], (NX, NY), jnp.float32) ** block_scale(part_splits[5], (NX, NY), ((0, 16),), -0.2, 0.2), -0.6, 0.4),
        "thickness": jnp.clip(1.9 + 0.6999999 * jax.random.uniform(part_splits[6], (NX, NY), jnp.float32) ** block_scale(part_splits[6], (NX, NY), ((0, 16),), -0.2, 0.2), 1.9, 2.6),
    }


flow_rate = 0.02
slide_rate = 0.1
diff_cap = 0.5
time_step = 0.4

def advance(height, base, friction, balance):
    hpad = jnp.pad(height, ((0, 0), (2, 2)))
    bpad = jnp.pad(base, ((0, 0), (2, 2)))
    fpad = jnp.pad(friction, ((0, 0), (2, 2)))
    surface = bpad + hpad
    grad_x = (surface[2:, 1:-1] - surface[:-2, 1:-1]) * 0.5
    grad_y = (surface[1:-1, 2:] - surface[1:-1, :-2]) * 0.5
    center = hpad[1:-1, 1:-1]
    fcent = fpad[1:-1, 1:-1]
    squared = center * center
    diff = flow_rate * squared * squared * center * (grad_x * grad_x + grad_y * grad_y)
    diff = jnp.minimum(diff + slide_rate * squared * jnp.exp(-fcent), diff_cap)
    scent = surface[1:-1, 1:-1]
    mid_d = diff[1:-1, 1:-1]
    mid_s = scent[1:-1, 1:-1]
    up_x = 0.5 * (diff[2:, 1:-1] + mid_d) * (scent[2:, 1:-1] - mid_s)
    down_x = 0.5 * (mid_d + diff[:-2, 1:-1]) * (mid_s - scent[:-2, 1:-1])
    up_y = 0.5 * (diff[1:-1, 2:] + mid_d) * (scent[1:-1, 2:] - mid_s)
    down_y = 0.5 * (mid_d + diff[1:-1, :-2]) * (mid_s - scent[1:-1, :-2])
    total = up_x - down_x + up_y - down_y
    return jnp.maximum(height[2:-2] + time_step * (total + balance[2:-2]), 0.0)

def reference(mode_fields, coeff, eigen, map_friction, bed, smb, thickness):
    weights = (coeff / jnp.sqrt(1.0 + eigen)).astype(jnp.bfloat16)
    flat = mode_fields.reshape(MODES, NX * NY)
    perturb = jnp.dot(weights[None, :], flat, preferred_element_type=jnp.float32).reshape(NX, NY)
    log_friction = map_friction + perturb
    rim = ((2, 2), (0, 0))
    base = jnp.pad(bed, rim)
    friction = jnp.pad(log_friction, rim)
    balance = jnp.pad(smb, rim)
    height = thickness
    for step in range(STEPS):
        height = advance(jnp.pad(height, rim), base, friction, balance)
    return (log_friction, height)
```

```python
import jax
import jax.numpy as jnp
from jax import lax
from jax.experimental import pallas as pl
from jax.experimental.pallas import tpu as pltpu
from jax.sharding import PartitionSpec as P

STEPS = 8
LANES = 128
GROUP = 8
LIMIT = 48

flow_rate = 0.02
slide_rate = 0.1
diff_cap = 0.5
time_step = 0.4


def lanes():
    return lax.broadcasted_iota(jnp.int32, (1, LANES), 1)


def fold(parts):
    parts, bit, lane = list(parts), 1, lanes()
    while bit < len(parts):
        high = (lane & bit) != 0
        for k in range(len(parts)):
            if k & bit == 0:
                x, y = parts[k], parts[k + bit]
                parts[k] = jnp.where(high, pltpu.roll(y, bit, 1), x)
                parts[k + bit] = jnp.where(high, y, pltpu.roll(x, LANES - bit, 1))
        bit *= 2
    return parts


def cut(ref, rows, blocks):
    return [ref[rows, k * LANES : (k + 1) * LANES] for k in range(blocks)]


def fold_all(*refs):
    out = refs[-1]
    blocks, rows = out.shape[1], out.shape[2]

    def tile(r, carry):
        at = pl.ds(pl.multiple_of(r * 8, 8), 8)
        for a, ref in enumerate(refs[:-1]):
            for p, part in enumerate(fold(cut(ref, at, blocks))):
                out[a, p, at, :] = part
        return carry

    lax.fori_loop(0, rows // 8, tile, 0)


def folded(*arrays):
    rows, columns = arrays[0].shape
    shape = (len(arrays), columns // LANES, rows, LANES)
    return pl.pallas_call(
        fold_all,
        out_shape=jax.ShapeDtypeStruct(shape, jnp.float32),
        compiler_params=pltpu.CompilerParams(vmem_limit_bytes=8 << 20),
        cost_estimate=pl.CostEstimate(flops=4 << 20, bytes_accessed=4 << 20, transcendentals=0),
    )(*arrays)


def slide_fold(friction, wide, narrow):
    blocks, rows = wide.shape[0], wide.shape[1]
    parts = fold([slide_rate * jnp.exp(-part) for part in cut(friction, slice(0, rows), blocks)])
    for p, part in enumerate(parts):
        wide[p] = part
        narrow[p] = part.astype(narrow.dtype)


def slides(friction):
    rows, columns = friction.shape
    shape = (columns // LANES, rows, LANES)
    return pl.pallas_call(
        slide_fold,
        out_shape=(jax.ShapeDtypeStruct(shape, jnp.float32), jax.ShapeDtypeStruct(shape, jnp.bfloat16)),
        compiler_params=pltpu.CompilerParams(vmem_limit_bytes=8 << 20),
    )(friction)


def weigh(own, coeff_ref, eigen_ref, fields, out, held, given, sems):
    strips, modes, rows, columns = held.shape
    me = lax.axis_index("modes")
    parity = me % 2 if own else 1 - me % 2

    def copy(p):
        row = (((me // 2) ^ p) * 2 + parity) * rows
        return pltpu.make_async_copy(
            fields.at[:, pl.ds(pl.multiple_of(row, rows), rows), :], held.at[p], sems.at[p]
        )

    small = [
        pltpu.make_async_copy(ref, given.at[i], sems.at[strips + i])
        for i, ref in enumerate((coeff_ref, eigen_ref))
    ]
    for one in small:
        one.start()

    def begin(p, carry):
        copy(p).start()
        return carry

    lax.fori_loop(0, strips, begin, 0)
    for one in small:
        one.wait()
    weights = given[0] / jnp.sqrt(1.0 + given[1])
    weights = weights.astype(jnp.bfloat16).astype(jnp.float32)
    at = lax.broadcasted_iota(jnp.int32, weights.shape, 1)
    scale = [
        jnp.sum(jnp.where(at == me * modes + k, weights, 0.0), axis=1, keepdims=True)
        for k in range(modes)
    ]

    def strip(p, carry):
        copy(p).wait()
        for b in range(columns // LANES):
            span = slice(b * LANES, (b + 1) * LANES)
            total = scale[0] * held[p, 0, :, span].astype(jnp.float32)
            for k in range(1, modes):
                total = total + scale[k] * held[p, k, :, span].astype(jnp.float32)
            out[p, :, span] = total.astype(out.dtype)
        return carry

    lax.fori_loop(0, strips, strip, 0)


def shares(coeff, eigen, mode_fields, rows, own, dtype):
    modes, total_rows, columns = mode_fields.shape
    strips = total_rows // rows // 2

    def kernel(*refs):
        weigh(own, *refs)

    return pl.pallas_call(
        kernel,
        in_specs=[pl.BlockSpec(memory_space=pl.ANY)] * 3,
        out_specs=pl.BlockSpec(memory_space=pltpu.VMEM),
        out_shape=jax.ShapeDtypeStruct((strips, rows, columns), dtype),
        scratch_shapes=[
            pltpu.VMEM((strips, modes, rows, columns), jnp.bfloat16),
            pltpu.VMEM((2,) + coeff.shape, jnp.float32),
            pltpu.SemaphoreType.DMA((strips + 2,)),
        ],
        compiler_params=pltpu.CompilerParams(vmem_limit_bytes=LIMIT << 20),
        cost_estimate=pl.CostEstimate(
            flops=modes * total_rows * columns,
            bytes_accessed=modes * total_rows * columns,
            transcendentals=0,
        ),
    )(coeff, eigen, mode_fields)


PAD = 8
NEVER = -1e30


def ice(peers, own_s, near_s, far_s, own_f, near_f, far_f, out, h0, s0, h1, s1, bed, bal, slide, diff):
    blocks, rows, _ = own_f.shape
    reach = 2 * STEPS
    extent = rows + 2 * reach
    me = lax.axis_index("modes")
    zero = jnp.minimum(me, 0)
    odd = me % 2 == 1
    above, below = me > 0, me < peers - 1
    mid_at = pl.ds(PAD + reach, rows)
    near_at = pl.ds(pl.multiple_of(PAD + jnp.where(odd, 0, rows + reach), 8), reach)
    far_at = pl.ds(pl.multiple_of(PAD + jnp.where(odd, rows + reach, 0), 8), reach)
    near_in = jnp.where(odd, above, below)
    far_in = jnp.where(odd, below, above)
    lane = lanes()

    def place_in(p, carry):
        slot = p + 2
        for src, at, inside in ((own_s, mid_at, True), (near_s, near_at, near_in), (far_s, far_at, far_in)):
            h, b, m = (src[a, p].astype(jnp.float32) for a in range(3))
            h0[slot, at, :] = h
            s0[slot, at, :] = h + b
            bed[slot, at, :] = b
            m = time_step * m
            bal[slot, at, :] = m if inside is True else jnp.where(inside, m, NEVER)
        for src, at in ((own_f, mid_at), (near_f, near_at), (far_f, far_at)):
            slide[slot, at, :] = src[p].astype(jnp.float32)
        return carry

    lax.fori_loop(0, blocks, place_in, 0, unroll=4)

    def wrap(ref, at, count):
        for q in range(count):
            x = ref[q + 2, at, :]
            x = jnp.where(
                lane >= LANES - blocks,
                jnp.where(lane == LANES - 1, 0.0, pltpu.roll(x, LANES - blocks - 1, 1)),
                pltpu.roll(x, LANES - blocks, 1),
            )
            ref[blocks + 2 + q, at, :] = x
            x = ref[blocks + 1 - q, at, :]
            x = jnp.where(
                lane < blocks,
                jnp.where(lane == 0, 0.0, pltpu.roll(x, blocks + 1, 1)),
                pltpu.roll(x, blocks, 1),
            )
            ref[1 - q, at, :] = x

    whole = pl.ds(PAD, extent)
    wrap(s0, whole, 2)
    wrap(h0, whole, 1)
    wrap(slide, whole, 1)

    for step in range(STEPS):
        h, s, hn, sn = (h0, s0, h1, s1) if step % 2 == 0 else (h1, s1, h0, s0)
        final = step == STEPS - 1
        edge = 2 * step + 2

        def window(first):
            low = first // 8 * 8
            at = pl.ds(PAD + low, extent - 2 * low)
            up = pl.ds(PAD + low - 1 + zero, extent - 2 * low)
            down = pl.ds(PAD + low + 1 + zero, extent - 2 * low)
            return at, up, down

        at, up, down = window(edge - 1)

        def diffuse(i, carry, h=h, s=s, at=at, up=up, down=down):
            for q in range(span):
                j = 1 + i * span + q
                gx = s[j, down, :] - s[j, up, :]
                gy = s[j + 1, at, :] - s[j - 1, at, :]
                thick = h[j, at, :]
                squared = thick * thick
                grad = (gx * gx + gy * gy) * (0.25 * flow_rate)
                diff[j, at, :] = jnp.minimum(squared * (squared * thick * grad + slide[j, at, :]), diff_cap)
            return carry

        span = (blocks + 2) // 2
        lax.fori_loop(0, 2, diffuse, 0)
        at, up, down = window(edge)

        def flow(i, carry, h=h, s=s, hn=hn, sn=sn, at=at, up=up, down=down, final=final):
            first = 2 + i * count
            s_mid, d_mid = s[first, at, :], diff[first, at, :]
            left = (diff[first - 1, at, :] + d_mid) * (s_mid - s[first - 1, at, :])
            for q in range(count):
                j = first + q
                s_next, d_next = s[j + 1, at, :], diff[j + 1, at, :]
                right = (d_mid + d_next) * (s_next - s_mid)
                total = right - left
                total += (diff[j, down, :] + d_mid) * (s[j, down, :] - s_mid)
                total -= (diff[j, up, :] + d_mid) * (s_mid - s[j, up, :])
                value = jnp.maximum(h[j, at, :] + (0.5 * time_step) * total + bal[j, at, :], 0.0)
                hn[j, at, :] = value
                if not final:
                    sn[j, at, :] = value + bed[j, at, :]
                left, s_mid, d_mid = right, s_next, d_next
            return carry

        count = min(GROUP, blocks)
        lax.fori_loop(0, blocks // count, flow, 0)
        if not final:
            wrap(sn, at, 2)
            wrap(hn, at, 1)

    h = h1 if STEPS % 2 else h0

    def tile(r, carry):
        at = pl.ds(pl.multiple_of(r * 8, 8), 8)
        from_at = pl.ds(pl.multiple_of(PAD + reach + r * 8, 8), 8)
        for k, part in enumerate(fold([h[p + 2, from_at, :] for p in range(blocks)])):
            out[at, k * LANES : (k + 1) * LANES] = part
        return carry

    lax.fori_loop(0, rows // 8, tile, 0)


def march(peers, own_s, near_s, far_s, own_f, near_f, far_f):
    blocks, rows, _ = own_f.shape
    vmem = pl.BlockSpec(memory_space=pltpu.VMEM)
    scratch = pltpu.VMEM((blocks + 4, rows + 4 * STEPS + 2 * PAD, LANES), jnp.float32)

    def kernel(*refs):
        ice(peers, *refs)

    return pl.pallas_call(
        kernel,
        in_specs=[vmem] * 6,
        out_specs=vmem,
        out_shape=jax.ShapeDtypeStruct((rows, blocks * LANES), jnp.float32),
        scratch_shapes=[scratch] * 8,
        compiler_params=pltpu.CompilerParams(vmem_limit_bytes=32 << 20),
    )(own_s, near_s, far_s, own_f, near_f, far_f)


def per_device(mode_fields, coeff, eigen, map_friction, bed, smb, thickness):
    peers = lax.axis_size("modes")
    rows, columns = map_friction.shape
    blocks = columns // LANES
    assert rows == 2 * STEPS and peers >= 2 and peers & (peers - 1) == 0
    assert peers >= 4 and columns % LANES == 0 and blocks & (blocks - 1) == 0 and 2 <= blocks <= LANES

    def swap(value, mask):
        return lax.ppermute(value, "modes", [(i, i ^ mask) for i in range(peers)])

    def across(value):
        pairs = [(i, i + 1) for i in range(1, peers - 1, 2)]
        return lax.ppermute(value, "modes", pairs + [(j, i) for i, j in pairs])

    given = shares(coeff[None], eigen[None], mode_fields, rows, False, jnp.bfloat16)
    kept = shares(coeff[None], eigen[None], mode_fields, rows, True, jnp.float32)
    total = kept + swap(given, 1).astype(jnp.float32)
    strips = total.shape[0]
    inner = min(strips, 4)
    taken = total[::inner]
    for part in [swap(total[k::inner].astype(jnp.float16), 2 * k) for k in reversed(range(1, inner))]:
        taken = taken + part.astype(jnp.float32)

    thickness, total = lax.optimization_barrier((thickness, total))
    statics = folded(thickness, bed, smb)
    sent = statics.astype(jnp.float16)
    near_s, far_s = swap(sent, 1).astype(jnp.float32), across(sent).astype(jnp.float32)

    while taken.shape[0] > 1:
        half = taken.shape[0] // 2
        taken = taken[:half] + swap(taken[half:].astype(jnp.float16), 2 * inner * half).astype(jnp.float32)
    log_friction = map_friction + taken[0]
    sliding, sent = slides(log_friction)
    far_f, near_f = across(sent), swap(sent, 1)
    height = march(peers, statics, near_s, far_s, sliding, near_f, far_f)
    return (log_friction, height)


def solution(mesh):
    return jax.shard_map(
        per_device,
        mesh=mesh,
        in_specs=(
            P(("groups", "modes"), None, None),
            P("groups"),
            P("groups"),
            P(("groups", "modes"), None),
            P(("groups", "modes"), None),
            P(("groups", "modes"), None),
            P(("groups", "modes"), None),
        ),
        out_specs=(P(("groups", "modes"), None), P(("groups", "modes"), None)),
        check_vma=False,
    )
```

```python
import jax
import jax.numpy as jnp
from jax import lax
from jax.experimental import pallas as pl
from jax.experimental.pallas import tpu as pltpu
from jax.sharding import PartitionSpec as P

STEPS = 8
LANES = 128
GROUP = 8
LIMIT = 48

flow_rate = 0.02
slide_rate = 0.1
diff_cap = 0.5
time_step = 0.4

unit = (0.25 * flow_rate * 0.5 * time_step) ** (1.0 / 7.0)
slide_unit = 0.5 * time_step * slide_rate / (unit * unit)
cap_unit = 0.5 * time_step * diff_cap


def lanes():
    return lax.broadcasted_iota(jnp.int32, (1, LANES), 1)


def fold(parts):
    parts, bit, lane = list(parts), 1, lanes()
    while bit < len(parts):
        high = (lane & bit) != 0
        for k in range(len(parts)):
            if k & bit == 0:
                x, y = parts[k], parts[k + bit]
                parts[k] = jnp.where(high, pltpu.roll(y, bit, 1), x)
                parts[k + bit] = jnp.where(high, y, pltpu.roll(x, LANES - bit, 1))
        bit *= 2
    return parts


def cut(ref, rows, blocks):
    return [ref[rows, k * LANES : (k + 1) * LANES] for k in range(blocks)]


def fold_all(*refs):
    out = refs[-1]
    blocks, rows = out.shape[1], out.shape[2]

    def tile(r, carry):
        at = pl.ds(pl.multiple_of(r * 8, 8), 8)
        for a, ref in enumerate(refs[:-1]):
            for p, part in enumerate(fold(cut(ref, at, blocks))):
                out[a, p, at, :] = part
        return carry

    lax.fori_loop(0, rows // 8, tile, 0)


def folded(*arrays):
    rows, columns = arrays[0].shape
    shape = (len(arrays), columns // LANES, rows, LANES)
    return pl.pallas_call(
        fold_all,
        out_shape=jax.ShapeDtypeStruct(shape, jnp.float32),
        compiler_params=pltpu.CompilerParams(vmem_limit_bytes=8 << 20),
        cost_estimate=pl.CostEstimate(flops=4 << 20, bytes_accessed=4 << 20, transcendentals=0),
    )(*arrays)


def slide_fold(friction, wide, narrow):
    blocks, rows = wide.shape[0], wide.shape[1]
    parts = fold([slide_unit * jnp.exp(-part) for part in cut(friction, slice(0, rows), blocks)])
    for p, part in enumerate(parts):
        wide[p] = part
        narrow[p] = part.astype(narrow.dtype)


def slides(friction):
    rows, columns = friction.shape
    shape = (columns // LANES, rows, LANES)
    return pl.pallas_call(
        slide_fold,
        out_shape=(jax.ShapeDtypeStruct(shape, jnp.float32), jax.ShapeDtypeStruct(shape, jnp.bfloat16)),
        compiler_params=pltpu.CompilerParams(vmem_limit_bytes=8 << 20),
    )(friction)


def weigh(own, coeff_ref, eigen_ref, fields, out, held, given, sems):
    strips, modes, rows, columns = held.shape
    me = lax.axis_index("modes")
    parity = me % 2 if own else 1 - me % 2

    def copy(p):
        row = (((me // 2) ^ p) * 2 + parity) * rows
        return pltpu.make_async_copy(
            fields.at[:, pl.ds(pl.multiple_of(row, rows), rows), :], held.at[p], sems.at[p]
        )

    small = [
        pltpu.make_async_copy(ref, given.at[i], sems.at[strips + i])
        for i, ref in enumerate((coeff_ref, eigen_ref))
    ]
    for one in small:
        one.start()

    def begin(p, carry):
        copy(p).start()
        return carry

    lax.fori_loop(0, strips, begin, 0)
    for one in small:
        one.wait()
    weights = given[0] / jnp.sqrt(1.0 + given[1])
    weights = weights.astype(jnp.bfloat16).astype(jnp.float32)
    at = lax.broadcasted_iota(jnp.int32, weights.shape, 1)
    scale = [
        jnp.sum(jnp.where(at == me * modes + k, weights, 0.0), axis=1, keepdims=True)
        for k in range(modes)
    ]

    def strip(p, carry):
        copy(p).wait()
        for b in range(columns // LANES):
            span = slice(b * LANES, (b + 1) * LANES)
            total = scale[0] * held[p, 0, :, span].astype(jnp.float32)
            for k in range(1, modes):
                total = total + scale[k] * held[p, k, :, span].astype(jnp.float32)
            out[p, :, span] = total.astype(out.dtype)
        return carry

    lax.fori_loop(0, strips, strip, 0)


def shares(coeff, eigen, mode_fields, rows, own, dtype):
    modes, total_rows, columns = mode_fields.shape
    strips = total_rows // rows // 2

    def kernel(*refs):
        weigh(own, *refs)

    return pl.pallas_call(
        kernel,
        in_specs=[pl.BlockSpec(memory_space=pltpu.HBM)] * 3,
        out_specs=pl.BlockSpec(memory_space=pltpu.VMEM),
        out_shape=jax.ShapeDtypeStruct((strips, rows, columns), dtype),
        scratch_shapes=[
            pltpu.VMEM((strips, modes, rows, columns), jnp.bfloat16),
            pltpu.VMEM((2,) + coeff.shape, jnp.float32),
            pltpu.SemaphoreType.DMA((strips + 2,)),
        ],
        compiler_params=pltpu.CompilerParams(vmem_limit_bytes=LIMIT << 20),
        cost_estimate=pl.CostEstimate(
            flops=modes * total_rows * columns,
            bytes_accessed=modes * total_rows * columns,
            transcendentals=0,
        ),
    )(coeff, eigen, mode_fields)


PAD = 8
NEVER = -1e30


def wrap(value, to_right, blocks):
    lane = lanes()
    if to_right:
        turned = jnp.where(
            lane >= LANES - blocks,
            pltpu.roll(value, LANES - blocks - 1, 1),
            pltpu.roll(value, LANES - blocks, 1),
        )
        return jnp.where(lane == LANES - 1, 0.0, turned)
    turned = jnp.where(lane < blocks, pltpu.roll(value, blocks + 1, 1), pltpu.roll(value, blocks, 1))
    return jnp.where(lane == 0, 0.0, turned)


def wrap_slots(ref, at, blocks, count):
    for q in range(count):
        ref[blocks + 2 + q, at, :] = wrap(ref[q + 2, at, :], True, blocks)
        ref[1 - q, at, :] = wrap(ref[blocks + 1 - q, at, :], False, blocks)


def spots(rows, reach):
    odd = lax.axis_index("modes") % 2 == 1
    near = pl.multiple_of(PAD + jnp.where(odd, 0, rows + reach), 8)
    far = pl.multiple_of(PAD + jnp.where(odd, rows + reach, 0), 8)
    return pl.ds(PAD + reach, rows), pl.ds(near, reach), pl.ds(far, reach)


def settle(peers, own_s, near_s, far_s, h0, s0, bed, bal):
    _, blocks, rows, _ = own_s.shape
    reach = 2 * STEPS
    me = lax.axis_index("modes")
    odd, above, below = me % 2 == 1, me > 0, me < peers - 1
    sides = (None, jnp.where(odd, above, below), jnp.where(odd, below, above))

    def block(p, carry):
        for src, at, inside in zip((own_s, near_s, far_s), spots(rows, reach), sides):
            h, b, m = (src[a, p] for a in range(3))
            h, b, m = unit * h, unit * b, (time_step * unit) * m
            h0[p + 2, at, :] = h
            s0[p + 2, at, :] = h + b
            bed[p + 2, at, :] = b
            bal[p + 2, at, :] = m if inside is None else jnp.where(inside, m, NEVER)
        return carry

    lax.fori_loop(0, blocks, block, 0, unroll=2)
    whole = pl.ds(PAD, rows + 2 * reach)
    wrap_slots(s0, whole, blocks, 2)
    wrap_slots(bed, whole, blocks, 1)
    wrap_slots(h0, whole, blocks, 1)


def settled(peers, own_s, near_s, far_s):
    _, blocks, rows, _ = own_s.shape
    shape = (blocks + 4, rows + 4 * STEPS + 2 * PAD, LANES)

    def kernel(*refs):
        settle(peers, *refs)

    return pl.pallas_call(
        kernel,
        out_shape=[jax.ShapeDtypeStruct(shape, jnp.float32)] * 4,
        compiler_params=pltpu.CompilerParams(vmem_limit_bytes=8 << 20),
        cost_estimate=pl.CostEstimate(flops=1, bytes_accessed=1, transcendentals=0),
    )(own_s, near_s, far_s)


def ice(own_f, near_f, far_f, h_in, s_in, bed, bal, out, h0, s0, h1, s1, slide, diff):
    blocks, rows, _ = own_f.shape
    reach = 2 * STEPS
    extent = rows + 2 * reach
    zero = jnp.minimum(lax.axis_index("modes"), 0)

    def block(p, carry):
        for src, at in zip((own_f, near_f, far_f), spots(rows, reach)):
            slide[p + 2, at, :] = src[p].astype(jnp.float32)
        return carry

    lax.fori_loop(0, blocks, block, 0, unroll=4)
    wrap_slots(slide, pl.ds(PAD, extent), blocks, 1)

    for step in range(STEPS):
        h, s = (h_in, s_in) if step == 0 else ((h0, s0), (h1, s1))[step % 2]
        hn, sn = ((h1, s1), (h0, s0))[step % 2]
        final = step == STEPS - 1
        edge = 2 * step + 2

        def window(first):
            count = -(-(extent - 2 * first) // 8) * 8
            return [pl.ds(PAD + first + off + zero, count) for off in (-1, 0, 1)]

        up, at, down = window(edge - 1)

        def diffuse(i, carry, h=h, s=s, at=at, up=up, down=down):
            for q in range(span):
                j = 1 + i * span + q
                gx = s[j, down, :] - s[j, up, :]
                gy = s[j + 1, at, :] - s[j - 1, at, :]
                thick = h[j, at, :]
                squared = thick * thick
                value = squared * (squared * thick * (gx * gx + gy * gy) + slide[j, at, :])
                diff[j, at, :] = jnp.minimum(value, cap_unit)
            return carry

        span = (blocks + 2) // 2
        lax.fori_loop(0, 2, diffuse, 0)
        up, at, down = window(edge)

        def flow(i, carry, h=h, s=s, hn=hn, sn=sn, at=at, up=up, down=down, final=final):
            first = 2 + i * count
            s_mid, d_mid = s[first, at, :], diff[first, at, :]
            left = (diff[first - 1, at, :] + d_mid) * (s_mid - s[first - 1, at, :])
            for q in range(count):
                j = first + q
                s_next, d_next = s[j + 1, at, :], diff[j + 1, at, :]
                right = (d_mid + d_next) * (s_next - s_mid)
                total = right - left
                total += (diff[j, down, :] + d_mid) * (s[j, down, :] - s_mid)
                total -= (diff[j, up, :] + d_mid) * (s_mid - s[j, up, :])
                value = jnp.maximum(h[j, at, :] + total + bal[j, at, :], 0.0)
                hn[j, at, :] = value
                if not final:
                    sn[j, at, :] = value + bed[j, at, :]
                left, s_mid, d_mid = right, s_next, d_next
            return carry

        count = min(GROUP, blocks)
        lax.fori_loop(0, blocks // count, flow, 0)
        if not final:
            wrap_slots(sn, at, blocks, 2)
            for slot in (1, blocks + 2):
                hn[slot, at, :] = sn[slot, at, :] - bed[slot, at, :]

    h = h1 if STEPS % 2 else h0

    def tile(r, carry):
        at = pl.ds(pl.multiple_of(r * 8, 8), 8)
        from_at = pl.ds(pl.multiple_of(PAD + reach + r * 8, 8), 8)
        for k, part in enumerate(fold([h[p + 2, from_at, :] * (1.0 / unit) for p in range(blocks)])):
            out[at, k * LANES : (k + 1) * LANES] = part
        return carry

    lax.fori_loop(0, rows // 8, tile, 0)


def march(own_f, near_f, far_f, *state):
    blocks, rows, _ = own_f.shape
    scratch = pltpu.VMEM(state[0].shape, jnp.float32)
    return pl.pallas_call(
        ice,
        out_shape=jax.ShapeDtypeStruct((rows, blocks * LANES), jnp.float32),
        scratch_shapes=[scratch] * 6,
        compiler_params=pltpu.CompilerParams(vmem_limit_bytes=32 << 20),
    )(own_f, near_f, far_f, *state)


def per_device(mode_fields, coeff, eigen, map_friction, bed, smb, thickness):
    peers = lax.axis_size("modes")
    rows, columns = map_friction.shape
    blocks = columns // LANES
    assert rows == 2 * STEPS and peers >= 2 and peers & (peers - 1) == 0
    assert peers >= 4 and columns % LANES == 0 and blocks & (blocks - 1) == 0 and 2 <= blocks <= LANES

    def swap(value, mask):
        return lax.ppermute(value, "modes", [(i, i ^ mask) for i in range(peers)])

    def across(value):
        pairs = [(i, i + 1) for i in range(1, peers - 1, 2)]
        return lax.ppermute(value, "modes", pairs + [(j, i) for i, j in pairs])

    coeff, eigen, mode_fields = (
        pltpu.with_memory_space_constraint(x, pltpu.HBM) for x in (coeff[None], eigen[None], mode_fields)
    )
    given = shares(coeff, eigen, mode_fields, rows, False, jnp.bfloat16)
    kept = shares(coeff, eigen, mode_fields, rows, True, jnp.float32)
    total = kept + swap(given, 1).astype(jnp.float32)
    strips = total.shape[0]
    inner = min(strips, 4)
    taken = total[::inner]
    for part in [swap(total[k::inner].astype(jnp.float16), 2 * k) for k in reversed(range(1, inner))]:
        taken = taken + part.astype(jnp.float32)

    thickness, total = lax.optimization_barrier((thickness, total))
    statics = folded(thickness, bed, smb)
    sent = statics.astype(jnp.float16)
    far_s, near_s = across(sent).astype(jnp.float32), swap(sent, 1).astype(jnp.float32)

    taken, sent = lax.optimization_barrier((taken, sent))
    while taken.shape[0] > 1:
        half = taken.shape[0] // 2
        taken = taken[:half] + swap(taken[half:].astype(jnp.float16), 2 * inner * half).astype(jnp.float32)
    log_friction = map_friction + taken[0]
    sliding, sent = slides(log_friction)
    far_f, near_f = across(sent), swap(sent, 1)
    state = settled(peers, statics, near_s, far_s)
    height = march(sliding, near_f, far_f, *state)
    return (log_friction, height)


def solution(mesh):
    return jax.shard_map(
        per_device,
        mesh=mesh,
        in_specs=(
            P(("groups", "modes"), None, None),
            P("groups"),
            P("groups"),
            P(("groups", "modes"), None),
            P(("groups", "modes"), None),
            P(("groups", "modes"), None),
            P(("groups", "modes"), None),
        ),
        out_specs=(P(("groups", "modes"), None), P(("groups", "modes"), None)),
        check_vma=False,
    )
```

```python
import jax
import jax.numpy as jnp
from jax import lax
from jax.experimental import pallas as pl
from jax.experimental.pallas import tpu as pltpu
from jax.sharding import PartitionSpec as P

STEPS = 8
LANES = 128
GROUP = 8
LIMIT = 48

flow_rate = 0.02
slide_rate = 0.1
diff_cap = 0.5
time_step = 0.4

unit = (0.25 * flow_rate * 0.5 * time_step) ** (1.0 / 7.0)
slide_unit = 0.5 * time_step * slide_rate / (unit * unit)
cap_unit = 0.5 * time_step * diff_cap


def lanes():
    return lax.broadcasted_iota(jnp.int32, (1, LANES), 1)


def fold(parts):
    parts, bit, lane = list(parts), 1, lanes()
    while bit < len(parts):
        high = (lane & bit) != 0
        for k in range(len(parts)):
            if k & bit == 0:
                x, y = parts[k], parts[k + bit]
                parts[k] = jnp.where(high, pltpu.roll(y, bit, 1), x)
                parts[k + bit] = jnp.where(high, y, pltpu.roll(x, LANES - bit, 1))
        bit *= 2
    return parts


def cut(ref, rows, blocks):
    return [ref[rows, k * LANES : (k + 1) * LANES] for k in range(blocks)]


def fold_all(*refs):
    out = refs[-1]
    blocks, rows = out.shape[1], out.shape[2]

    def tile(r, carry):
        at = pl.ds(pl.multiple_of(r * 8, 8), 8)
        for a, ref in enumerate(refs[:-1]):
            for p, part in enumerate(fold(cut(ref, at, blocks))):
                out[a, p, at, :] = part
        return carry

    lax.fori_loop(0, rows // 8, tile, 0)


def folded(*arrays):
    rows, columns = arrays[0].shape
    shape = (len(arrays), columns // LANES, rows, LANES)
    return pl.pallas_call(
        fold_all,
        out_shape=jax.ShapeDtypeStruct(shape, jnp.float32),
        compiler_params=pltpu.CompilerParams(vmem_limit_bytes=8 << 20),
        cost_estimate=pl.CostEstimate(flops=4 << 20, bytes_accessed=4 << 20, transcendentals=0),
    )(*arrays)


def slide_fold(friction, wide, narrow):
    blocks, rows = wide.shape[0], wide.shape[1]
    parts = fold([slide_unit * jnp.exp(-part) for part in cut(friction, slice(0, rows), blocks)])
    for p, part in enumerate(parts):
        wide[p] = part
        narrow[p] = part.astype(narrow.dtype)


def slides(friction):
    rows, columns = friction.shape
    shape = (columns // LANES, rows, LANES)
    return pl.pallas_call(
        slide_fold,
        out_shape=(jax.ShapeDtypeStruct(shape, jnp.float32), jax.ShapeDtypeStruct(shape, jnp.bfloat16)),
        compiler_params=pltpu.CompilerParams(vmem_limit_bytes=8 << 20),
    )(friction)


def direct(strips):
    return min(strips, 4)


def pair_at(i, strips):
    together = strips // direct(strips)
    return (i % together) * direct(strips) + i // together


def weigh(own, coeff_ref, eigen_ref, fields, out, held, given, sems):
    strips, modes, rows, columns = held.shape
    me = lax.axis_index("modes")
    parity = me % 2 if own else 1 - me % 2

    def copy(p):
        row = (((me // 2) ^ pair_at(p, strips)) * 2 + parity) * rows
        return pltpu.make_async_copy(
            fields.at[:, pl.ds(pl.multiple_of(row, rows), rows), :], held.at[p], sems.at[p]
        )

    small = [
        pltpu.make_async_copy(ref, given.at[i], sems.at[strips + i])
        for i, ref in enumerate((coeff_ref, eigen_ref))
    ]
    for one in small:
        one.start()

    def begin(p, carry):
        copy(p).start()
        return carry

    lax.fori_loop(0, strips, begin, 0)
    for one in small:
        one.wait()
    weights = given[0] / jnp.sqrt(1.0 + given[1])
    weights = weights.astype(jnp.bfloat16).astype(jnp.float32)
    at = lax.broadcasted_iota(jnp.int32, weights.shape, 1)
    scale = [
        jnp.sum(jnp.where(at == me * modes + k, weights, 0.0), axis=1, keepdims=True)
        for k in range(modes)
    ]

    def strip(p, carry):
        copy(p).wait()
        for b in range(columns // LANES):
            span = slice(b * LANES, (b + 1) * LANES)
            total = scale[0] * held[p, 0, :, span].astype(jnp.float32)
            for k in range(1, modes):
                total = total + scale[k] * held[p, k, :, span].astype(jnp.float32)
            out[p, :, span] = total.astype(out.dtype)
        return carry

    lax.fori_loop(0, strips, strip, 0)


def shares(coeff, eigen, mode_fields, rows, own, dtype):
    modes, total_rows, columns = mode_fields.shape
    strips = total_rows // rows // 2

    def kernel(*refs):
        weigh(own, *refs)

    return pl.pallas_call(
        kernel,
        in_specs=[pl.BlockSpec(memory_space=pltpu.HBM)] * 3,
        out_specs=pl.BlockSpec(memory_space=pltpu.VMEM),
        out_shape=jax.ShapeDtypeStruct((strips, rows, columns), dtype),
        scratch_shapes=[
            pltpu.VMEM((strips, modes, rows, columns), jnp.bfloat16),
            pltpu.VMEM((2,) + coeff.shape, jnp.float32),
            pltpu.SemaphoreType.DMA((strips + 2,)),
        ],
        compiler_params=pltpu.CompilerParams(vmem_limit_bytes=LIMIT << 20),
        cost_estimate=pl.CostEstimate(
            flops=modes * total_rows * columns,
            bytes_accessed=modes * total_rows * columns,
            transcendentals=0,
        ),
    )(coeff, eigen, mode_fields)


PAD = 8
NEVER = -1e30


def wrap(value, to_right, blocks):
    lane = lanes()
    if to_right:
        turned = jnp.where(
            lane >= LANES - blocks,
            pltpu.roll(value, LANES - blocks - 1, 1),
            pltpu.roll(value, LANES - blocks, 1),
        )
        return jnp.where(lane == LANES - 1, 0.0, turned)
    turned = jnp.where(lane < blocks, pltpu.roll(value, blocks + 1, 1), pltpu.roll(value, blocks, 1))
    return jnp.where(lane == 0, 0.0, turned)


def wrap_slots(ref, at, blocks, count):
    for q in range(count):
        ref[blocks + 2 + q, at, :] = wrap(ref[q + 2, at, :], True, blocks)
        ref[1 - q, at, :] = wrap(ref[blocks + 1 - q, at, :], False, blocks)


def spots(rows, reach):
    odd = lax.axis_index("modes") % 2 == 1
    near = pl.multiple_of(PAD + jnp.where(odd, 0, rows + reach), 8)
    far = pl.multiple_of(PAD + jnp.where(odd, rows + reach, 0), 8)
    return pl.ds(PAD + reach, rows), pl.ds(near, reach), pl.ds(far, reach)


def settle(peers, own_s, near_s, far_s, h0, s0, bed, bal, square, steep):
    _, blocks, rows, _ = own_s.shape
    reach = 2 * STEPS
    me = lax.axis_index("modes")
    odd, above, below = me % 2 == 1, me > 0, me < peers - 1
    sides = (None, jnp.where(odd, above, below), jnp.where(odd, below, above))

    def block(p, carry):
        for src, at, inside in zip((own_s, near_s, far_s), spots(rows, reach), sides):
            h, b, m = (src[a, p] for a in range(3))
            h, b, m = unit * h, unit * b, (time_step * unit) * m
            h0[p + 2, at, :] = h
            s0[p + 2, at, :] = h + b
            bed[p + 2, at, :] = b
            bal[p + 2, at, :] = m if inside is None else jnp.where(inside, m, NEVER)
        return carry

    lax.fori_loop(0, blocks, block, 0, unroll=2)
    whole = pl.ds(PAD, rows + 2 * reach)
    wrap_slots(s0, whole, blocks, 2)
    wrap_slots(bed, whole, blocks, 1)
    wrap_slots(h0, whole, blocks, 1)
    zero = jnp.minimum(me, 0)
    up, down = (pl.ds(PAD + off + zero, rows + 2 * reach) for off in (-1, 1))

    def flux(i, carry):
        for q in range((blocks + 2) // 2):
            j = 1 + i * ((blocks + 2) // 2) + q
            gx = s0[j, down, :] - s0[j, up, :]
            gy = s0[j + 1, whole, :] - s0[j - 1, whole, :]
            thick = h0[j, whole, :]
            squared = thick * thick
            square[j, whole, :] = squared
            steep[j, whole, :] = squared * (squared * thick * (gx * gx + gy * gy))
        return carry

    lax.fori_loop(0, 2, flux, 0)


def settled(peers, own_s, near_s, far_s):
    _, blocks, rows, _ = own_s.shape
    shape = (blocks + 4, rows + 4 * STEPS + 2 * PAD, LANES)

    def kernel(*refs):
        settle(peers, *refs)

    return pl.pallas_call(
        kernel,
        out_shape=[jax.ShapeDtypeStruct(shape, jnp.float32)] * 6,
        compiler_params=pltpu.CompilerParams(vmem_limit_bytes=8 << 20),
        cost_estimate=pl.CostEstimate(flops=1, bytes_accessed=1, transcendentals=0),
    )(own_s, near_s, far_s)


def ice(own_f, near_f, far_f, h_in, s_in, bed, bal, square, steep, out, h0, s0, h1, s1, slide, diff):
    blocks, rows, _ = own_f.shape
    reach = 2 * STEPS
    extent = rows + 2 * reach
    zero = jnp.minimum(lax.axis_index("modes"), 0)

    def block(p, carry):
        for src, at in zip((own_f, near_f, far_f), spots(rows, reach)):
            slide[p + 2, at, :] = src[p].astype(jnp.float32)
        return carry

    lax.fori_loop(0, blocks, block, 0, unroll=4)
    wrap_slots(slide, pl.ds(PAD, extent), blocks, 1)

    for step in range(STEPS):
        h, s = (h_in, s_in) if step == 0 else ((h0, s0), (h1, s1))[step % 2]
        hn, sn = ((h1, s1), (h0, s0))[step % 2]
        final = step == STEPS - 1
        edge = 2 * step + 2

        def window(first):
            count = -(-(extent - 2 * first) // 8) * 8
            return [pl.ds(PAD + first + off + zero, count) for off in (-1, 0, 1)]

        up, at, down = window(edge - 1)

        def diffuse(h=h, s=s, at=at, up=up, down=down, step=step):
            for j in range(1, blocks + 3):
                if step == 0:
                    diff[j, at, :] = jnp.minimum(steep[j, at, :] + square[j, at, :] * slide[j, at, :], cap_unit)
                    continue
                gx = s[j, down, :] - s[j, up, :]
                gy = s[j + 1, at, :] - s[j - 1, at, :]
                thick = h[j, at, :]
                squared = thick * thick
                value = squared * (squared * thick * (gx * gx + gy * gy) + slide[j, at, :])
                diff[j, at, :] = jnp.minimum(value, cap_unit)

        diffuse()
        up, at, down = window(edge)

        def flow(i, carry, h=h, s=s, hn=hn, sn=sn, at=at, up=up, down=down, final=final):
            first = 2 + i * count
            s_mid, d_mid = s[first, at, :], diff[first, at, :]
            left = (diff[first - 1, at, :] + d_mid) * (s_mid - s[first - 1, at, :])
            for q in range(count):
                j = first + q
                s_next, d_next = s[j + 1, at, :], diff[j + 1, at, :]
                right = (d_mid + d_next) * (s_next - s_mid)
                total = right - left
                total += (diff[j, down, :] + d_mid) * (s[j, down, :] - s_mid)
                total -= (diff[j, up, :] + d_mid) * (s_mid - s[j, up, :])
                value = jnp.maximum(h[j, at, :] + total + bal[j, at, :], 0.0)
                hn[j, at, :] = value
                if not final:
                    sn[j, at, :] = value + bed[j, at, :]
                left, s_mid, d_mid = right, s_next, d_next
            return carry

        count = min(GROUP, blocks)
        lax.fori_loop(0, blocks // count, flow, 0)
        if not final:
            wrap_slots(sn, at, blocks, 2)
            for slot in (1, blocks + 2):
                hn[slot, at, :] = sn[slot, at, :] - bed[slot, at, :]

    h = h1 if STEPS % 2 else h0

    def tile(r, carry):
        at = pl.ds(pl.multiple_of(r * 8, 8), 8)
        from_at = pl.ds(pl.multiple_of(PAD + reach + r * 8, 8), 8)
        for k, part in enumerate(fold([h[p + 2, from_at, :] * (1.0 / unit) for p in range(blocks)])):
            out[at, k * LANES : (k + 1) * LANES] = part
        return carry

    lax.fori_loop(0, rows // 8, tile, 0, unroll=2)


def march(own_f, near_f, far_f, *state):
    blocks, rows, _ = own_f.shape
    scratch = pltpu.VMEM(state[0].shape, jnp.float32)
    return pl.pallas_call(
        ice,
        out_shape=jax.ShapeDtypeStruct((rows, blocks * LANES), jnp.float32),
        scratch_shapes=[scratch] * 6,
        compiler_params=pltpu.CompilerParams(vmem_limit_bytes=32 << 20),
    )(own_f, near_f, far_f, *state)


def per_device(mode_fields, coeff, eigen, map_friction, bed, smb, thickness):
    peers = lax.axis_size("modes")
    rows, columns = map_friction.shape
    blocks = columns // LANES
    assert rows == 2 * STEPS and peers >= 2 and peers & (peers - 1) == 0
    assert peers >= 4 and columns % LANES == 0 and blocks & (blocks - 1) == 0 and 2 <= blocks <= LANES

    def swap(value, mask):
        return lax.ppermute(value, "modes", [(i, i ^ mask) for i in range(peers)])

    def across(value):
        pairs = [(i, i + 1) for i in range(1, peers - 1, 2)]
        return lax.ppermute(value, "modes", pairs + [(j, i) for i, j in pairs])

    coeff, eigen, mode_fields = (
        pltpu.with_memory_space_constraint(x, pltpu.HBM) for x in (coeff[None], eigen[None], mode_fields)
    )
    given = shares(coeff, eigen, mode_fields, rows, False, jnp.bfloat16)
    kept = shares(coeff, eigen, mode_fields, rows, True, jnp.float32)
    arrived = swap(given, 1)
    strips = kept.shape[0]
    inner = direct(strips)

    def summed(k):
        at = slice(k * (strips // inner), (k + 1) * (strips // inner))
        return kept[at] + arrived[at].astype(jnp.float32)

    taken = summed(0)
    for part in [swap(summed(k).astype(jnp.float16), 2 * k) for k in reversed(range(1, inner))]:
        taken = taken + part.astype(jnp.float32)

    thickness, arrived = lax.optimization_barrier((thickness, arrived))
    statics = folded(thickness, bed, smb)
    sent = statics.astype(jnp.float16)
    far_s, near_s = across(sent).astype(jnp.float32), swap(sent, 1).astype(jnp.float32)

    taken, sent = lax.optimization_barrier((taken, sent))
    while taken.shape[0] > 1:
        half = taken.shape[0] // 2
        taken = taken[:half] + swap(taken[half:].astype(jnp.float16), 2 * inner * half).astype(jnp.float32)
    log_friction = map_friction + taken[0]
    sliding, sent = slides(log_friction)
    far_f, near_f = across(sent), swap(sent, 1)
    state = settled(peers, statics, near_s, far_s)
    height = march(sliding, near_f, far_f, *state)
    return (log_friction, height)


def solution(mesh):
    return jax.shard_map(
        per_device,
        mesh=mesh,
        in_specs=(
            P(("groups", "modes"), None, None),
            P("groups"),
            P("groups"),
            P(("groups", "modes"), None),
            P(("groups", "modes"), None),
            P(("groups", "modes"), None),
            P(("groups", "modes"), None),
        ),
        out_specs=(P(("groups", "modes"), None), P(("groups", "modes"), None)),
        check_vma=False,
    )
```

```python
import jax
import jax.numpy as jnp
from jax import lax
from jax.experimental import pallas as pl
from jax.experimental.pallas import tpu as pltpu
from jax.sharding import PartitionSpec as P

STEPS = 8
LANES = 128
GROUP = 8
LIMIT = 48

flow_rate = 0.02
slide_rate = 0.1
diff_cap = 0.5
time_step = 0.4

unit = (0.25 * flow_rate * 0.5 * time_step) ** (1.0 / 7.0)
slide_unit = 0.5 * time_step * slide_rate / (unit * unit)
cap_unit = 0.5 * time_step * diff_cap


def lanes():
    return lax.broadcasted_iota(jnp.int32, (1, LANES), 1)


def fold(parts):
    parts, bit, lane = list(parts), 1, lanes()
    while bit < len(parts):
        high = (lane & bit) != 0
        for k in range(len(parts)):
            if k & bit == 0:
                x, y = parts[k], parts[k + bit]
                parts[k] = jnp.where(high, pltpu.roll(y, bit, 1), x)
                parts[k + bit] = jnp.where(high, y, pltpu.roll(x, LANES - bit, 1))
        bit *= 2
    return parts


def cut(ref, rows, blocks):
    return [ref[rows, k * LANES : (k + 1) * LANES] for k in range(blocks)]


def fold_all(*refs):
    out = refs[-1]
    blocks, rows = out.shape[1], out.shape[2]

    def tile(r, carry):
        at = pl.ds(pl.multiple_of(r * 8, 8), 8)
        for a, ref in enumerate(refs[:-1]):
            for p, part in enumerate(fold(cut(ref, at, blocks))):
                out[a, p, at, :] = part
        return carry

    lax.fori_loop(0, rows // 8, tile, 0)


def folded(*arrays):
    rows, columns = arrays[0].shape
    shape = (len(arrays), columns // LANES, rows, LANES)
    return pl.pallas_call(
        fold_all,
        out_shape=jax.ShapeDtypeStruct(shape, jnp.float32),
        compiler_params=pltpu.CompilerParams(vmem_limit_bytes=8 << 20),
        cost_estimate=pl.CostEstimate(flops=4 << 20, bytes_accessed=4 << 20, transcendentals=0),
    )(*arrays)


def slide_fold(friction, wide, narrow):
    blocks, rows = wide.shape[0], wide.shape[1]
    parts = fold([slide_unit * jnp.exp(-part) for part in cut(friction, slice(0, rows), blocks)])
    for p, part in enumerate(parts):
        wide[p] = part
        narrow[p] = part.astype(narrow.dtype)


def slides(friction):
    rows, columns = friction.shape
    shape = (columns // LANES, rows, LANES)
    return pl.pallas_call(
        slide_fold,
        out_shape=(jax.ShapeDtypeStruct(shape, jnp.float32), jax.ShapeDtypeStruct(shape, jnp.bfloat16)),
        compiler_params=pltpu.CompilerParams(vmem_limit_bytes=8 << 20),
    )(friction)


def direct(strips):
    return min(strips, 4)


def partner(slot, odd):
    other = slot if slot in (0, 3) else 3 - slot
    return other if odd else slot


def pair_at(i, strips, parity):
    together = strips // direct(strips)
    slot = i // together
    if direct(strips) == 4:
        middle = jnp.logical_and(slot > 0, slot < 3)
        slot = jnp.where(jnp.logical_and(middle, parity == 1), 3 - slot, slot)
    return (i % together) * direct(strips) + slot


def weigh(own, coeff_ref, eigen_ref, fields, out, held, given, sems):
    strips, modes, rows, columns = held.shape
    me = lax.axis_index("modes")
    parity = me % 2 if own else 1 - me % 2

    def copy(p):
        row = (((me // 2) ^ pair_at(p, strips, parity)) * 2 + parity) * rows
        return pltpu.make_async_copy(
            fields.at[:, pl.ds(pl.multiple_of(row, rows), rows), :], held.at[p], sems.at[p]
        )

    small = [
        pltpu.make_async_copy(ref, given.at[i], sems.at[strips + i])
        for i, ref in enumerate((coeff_ref, eigen_ref))
    ]
    for one in small:
        one.start()

    def begin(p, carry):
        copy(p).start()
        return carry

    lax.fori_loop(0, strips, begin, 0)
    for one in small:
        one.wait()
    weights = given[0] / jnp.sqrt(1.0 + given[1])
    weights = weights.astype(jnp.bfloat16).astype(jnp.float32)
    at = lax.broadcasted_iota(jnp.int32, weights.shape, 1)
    scale = [
        jnp.sum(jnp.where(at == me * modes + k, weights, 0.0), axis=1, keepdims=True)
        for k in range(modes)
    ]

    def strip(p, carry):
        copy(p).wait()
        for b in range(columns // LANES):
            span = slice(b * LANES, (b + 1) * LANES)
            total = scale[0] * held[p, 0, :, span].astype(jnp.float32)
            for k in range(1, modes):
                total = total + scale[k] * held[p, k, :, span].astype(jnp.float32)
            out[p, :, span] = total.astype(out.dtype)
        return carry

    lax.fori_loop(0, strips, strip, 0)


def shares(coeff, eigen, mode_fields, rows, own, dtype):
    modes, total_rows, columns = mode_fields.shape
    strips = total_rows // rows // 2

    def kernel(*refs):
        weigh(own, *refs)

    return pl.pallas_call(
        kernel,
        in_specs=[pl.BlockSpec(memory_space=pltpu.HBM)] * 3,
        out_specs=pl.BlockSpec(memory_space=pltpu.VMEM),
        out_shape=jax.ShapeDtypeStruct((strips, rows, columns), dtype),
        scratch_shapes=[
            pltpu.VMEM((strips, modes, rows, columns), jnp.bfloat16),
            pltpu.VMEM((2,) + coeff.shape, jnp.float32),
            pltpu.SemaphoreType.DMA((strips + 2,)),
        ],
        compiler_params=pltpu.CompilerParams(vmem_limit_bytes=LIMIT << 20),
        cost_estimate=pl.CostEstimate(
            flops=modes * total_rows * columns,
            bytes_accessed=modes * total_rows * columns,
            transcendentals=0,
        ),
    )(coeff, eigen, mode_fields)


PAD = 8
NEVER = -1e30


def wrap(value, to_right, blocks):
    lane = lanes()
    if to_right:
        turned = jnp.where(
            lane >= LANES - blocks,
            pltpu.roll(value, LANES - blocks - 1, 1),
            pltpu.roll(value, LANES - blocks, 1),
        )
        return jnp.where(lane == LANES - 1, 0.0, turned)
    turned = jnp.where(lane < blocks, pltpu.roll(value, blocks + 1, 1), pltpu.roll(value, blocks, 1))
    return jnp.where(lane == 0, 0.0, turned)


def wrap_slots(ref, at, blocks, count):
    for q in range(count):
        ref[blocks + 2 + q, at, :] = wrap(ref[q + 2, at, :], True, blocks)
        ref[1 - q, at, :] = wrap(ref[blocks + 1 - q, at, :], False, blocks)


def spots(rows, reach):
    odd = lax.axis_index("modes") % 2 == 1
    near = pl.multiple_of(PAD + jnp.where(odd, 0, rows + reach), 8)
    far = pl.multiple_of(PAD + jnp.where(odd, rows + reach, 0), 8)
    return pl.ds(PAD + reach, rows), pl.ds(near, reach), pl.ds(far, reach)


def settle(peers, own_s, near_s, far_s, h0, s0, bed, bal, square, steep):
    _, blocks, rows, _ = own_s.shape
    reach = 2 * STEPS
    me = lax.axis_index("modes")
    odd, above, below = me % 2 == 1, me > 0, me < peers - 1
    sides = (None, jnp.where(odd, above, below), jnp.where(odd, below, above))

    def block(p, carry):
        for src, at, inside in zip((own_s, near_s, far_s), spots(rows, reach), sides):
            h, b, m = (src[a, p] for a in range(3))
            h, b, m = unit * h, unit * b, (time_step * unit) * m
            h0[p + 2, at, :] = h
            s0[p + 2, at, :] = h + b
            bed[p + 2, at, :] = b
            bal[p + 2, at, :] = m if inside is None else jnp.where(inside, m, NEVER)
        return carry

    lax.fori_loop(0, blocks, block, 0, unroll=2)
    whole = pl.ds(PAD, rows + 2 * reach)
    wrap_slots(s0, whole, blocks, 2)
    wrap_slots(bed, whole, blocks, 1)
    wrap_slots(h0, whole, blocks, 1)
    zero = jnp.minimum(me, 0)
    up, down = (pl.ds(PAD + off + zero, rows + 2 * reach) for off in (-1, 1))

    def flux(i, carry):
        for q in range((blocks + 2) // 2):
            j = 1 + i * ((blocks + 2) // 2) + q
            gx = s0[j, down, :] - s0[j, up, :]
            gy = s0[j + 1, whole, :] - s0[j - 1, whole, :]
            thick = h0[j, whole, :]
            squared = thick * thick
            square[j, whole, :] = squared
            steep[j, whole, :] = squared * (squared * thick * (gx * gx + gy * gy))
        return carry

    lax.fori_loop(0, 2, flux, 0)


def settled(peers, own_s, near_s, far_s):
    _, blocks, rows, _ = own_s.shape
    shape = (blocks + 4, rows + 4 * STEPS + 2 * PAD, LANES)

    def kernel(*refs):
        settle(peers, *refs)

    return pl.pallas_call(
        kernel,
        out_shape=[jax.ShapeDtypeStruct(shape, jnp.float32)] * 6,
        compiler_params=pltpu.CompilerParams(vmem_limit_bytes=8 << 20),
        cost_estimate=pl.CostEstimate(flops=1, bytes_accessed=1, transcendentals=0),
    )(own_s, near_s, far_s)


def ice(own_f, near_f, far_f, h_in, s_in, bed, bal, square, steep, out, h0, s0, h1, s1, slide, diff):
    blocks, rows, _ = own_f.shape
    reach = 2 * STEPS
    extent = rows + 2 * reach
    zero = jnp.minimum(lax.axis_index("modes"), 0)

    def block(p, carry):
        for src, at in zip((own_f, near_f, far_f), spots(rows, reach)):
            slide[p + 2, at, :] = src[p].astype(jnp.float32)
        return carry

    lax.fori_loop(0, blocks, block, 0, unroll=4)
    wrap_slots(slide, pl.ds(PAD, extent), blocks, 1)

    for step in range(STEPS):
        h, s = (h_in, s_in) if step == 0 else ((h0, s0), (h1, s1))[step % 2]
        hn, sn = ((h1, s1), (h0, s0))[step % 2]
        final = step == STEPS - 1
        edge = 2 * step + 2

        def window(first):
            count = -(-(extent - 2 * first) // 8) * 8
            return [pl.ds(PAD + first + off + zero, count) for off in (-1, 0, 1)]

        up, at, down = window(edge - 1)

        def diffuse(h=h, s=s, at=at, up=up, down=down, step=step):
            for j in range(1, blocks + 3):
                if step == 0:
                    diff[j, at, :] = jnp.minimum(steep[j, at, :] + square[j, at, :] * slide[j, at, :], cap_unit)
                    continue
                gx = s[j, down, :] - s[j, up, :]
                gy = s[j + 1, at, :] - s[j - 1, at, :]
                thick = h[j, at, :]
                squared = thick * thick
                value = squared * (squared * thick * (gx * gx + gy * gy) + slide[j, at, :])
                diff[j, at, :] = jnp.minimum(value, cap_unit)

        diffuse()
        up, at, down = window(edge)

        def flow(i, carry, h=h, s=s, hn=hn, sn=sn, at=at, up=up, down=down, final=final):
            first = 2 + i * count
            s_mid, d_mid = s[first, at, :], diff[first, at, :]
            left = (diff[first - 1, at, :] + d_mid) * (s_mid - s[first - 1, at, :])
            for q in range(count):
                j = first + q
                s_next, d_next = s[j + 1, at, :], diff[j + 1, at, :]
                right = (d_mid + d_next) * (s_next - s_mid)
                total = right - left
                total += (diff[j, down, :] + d_mid) * (s[j, down, :] - s_mid)
                total -= (diff[j, up, :] + d_mid) * (s_mid - s[j, up, :])
                value = jnp.maximum(h[j, at, :] + total + bal[j, at, :], 0.0)
                hn[j, at, :] = value
                if not final:
                    sn[j, at, :] = value + bed[j, at, :]
                left, s_mid, d_mid = right, s_next, d_next
            return carry

        count = min(GROUP, blocks)
        lax.fori_loop(0, blocks // count, flow, 0)
        if not final:
            wrap_slots(sn, at, blocks, 2)
            for slot in (1, blocks + 2):
                hn[slot, at, :] = sn[slot, at, :] - bed[slot, at, :]

    h = h1 if STEPS % 2 else h0

    def tile(r, carry):
        at = pl.ds(pl.multiple_of(r * 8, 8), 8)
        from_at = pl.ds(pl.multiple_of(PAD + reach + r * 8, 8), 8)
        for k, part in enumerate(fold([h[p + 2, from_at, :] * (1.0 / unit) for p in range(blocks)])):
            out[at, k * LANES : (k + 1) * LANES] = part
        return carry

    lax.fori_loop(0, rows // 8, tile, 0, unroll=2)


def march(own_f, near_f, far_f, *state):
    blocks, rows, _ = own_f.shape
    scratch = pltpu.VMEM(state[0].shape, jnp.float32)
    return pl.pallas_call(
        ice,
        out_shape=jax.ShapeDtypeStruct((rows, blocks * LANES), jnp.float32),
        scratch_shapes=[scratch] * 6,
        compiler_params=pltpu.CompilerParams(vmem_limit_bytes=32 << 20),
    )(own_f, near_f, far_f, *state)


def per_device(mode_fields, coeff, eigen, map_friction, bed, smb, thickness):
    peers = lax.axis_size("modes")
    rows, columns = map_friction.shape
    blocks = columns // LANES
    assert rows == 2 * STEPS and peers >= 2 and peers & (peers - 1) == 0
    assert peers >= 4 and columns % LANES == 0 and blocks & (blocks - 1) == 0 and 2 <= blocks <= LANES

    def swap(value, mask):
        return lax.ppermute(value, "modes", [(i, i ^ mask) for i in range(peers)])

    def across(value):
        pairs = [(i, i + 1) for i in range(1, peers - 1, 2)]
        return lax.ppermute(value, "modes", pairs + [(j, i) for i, j in pairs])

    coeff, eigen, mode_fields = (
        pltpu.with_memory_space_constraint(x, pltpu.HBM) for x in (coeff[None], eigen[None], mode_fields)
    )
    given = shares(coeff, eigen, mode_fields, rows, False, jnp.bfloat16)
    kept = shares(coeff, eigen, mode_fields, rows, True, jnp.float32)
    arrived = swap(given, 1)
    strips = kept.shape[0]
    inner = direct(strips)

    def summed(k):
        at = slice(k * (strips // inner), (k + 1) * (strips // inner))
        return kept[at] + arrived[at].astype(jnp.float32)

    def exchanged(many):
        found = summed(0)[many]
        for k in (1, 2, 3) if inner == 4 else range(1, inner):
            pairs = [(i, i ^ (2 * (partner(k, i % 2) if inner == 4 else k))) for i in range(peers)]
            part = lax.ppermute(summed(k)[many].astype(jnp.float16), "modes", pairs)
            found = found + part.astype(jnp.float32)
        return found

    together = strips // inner
    half = together // 2
    onward = exchanged(slice(half, together)) if half else None
    taken = exchanged(slice(0, max(half, 1)))

    thickness, arrived = lax.optimization_barrier((thickness, arrived))
    statics = folded(thickness, bed, smb)
    sent = statics.astype(jnp.float16)
    far_s, near_s = across(sent).astype(jnp.float32), swap(sent, 1).astype(jnp.float32)

    onward, sent = lax.optimization_barrier((onward, sent))
    while half:
        taken = taken + swap(onward.astype(jnp.float16), 2 * inner * half).astype(jnp.float32)
        half //= 2
        taken, onward = taken[: max(half, 1)], taken[half:]
    log_friction = map_friction + taken[0]
    sliding, sent = slides(log_friction)
    far_f, near_f = across(sent), swap(sent, 1)
    state = settled(peers, statics, near_s, far_s)
    height = march(sliding, near_f, far_f, *state)
    return (log_friction, height)


def solution(mesh):
    return jax.shard_map(
        per_device,
        mesh=mesh,
        in_specs=(
            P(("groups", "modes"), None, None),
            P("groups"),
            P("groups"),
            P(("groups", "modes"), None),
            P(("groups", "modes"), None),
            P(("groups", "modes"), None),
            P(("groups", "modes"), None),
        ),
        out_specs=(P(("groups", "modes"), None), P(("groups", "modes"), None)),
        check_vma=False,
    )
```

```python
import jax
import jax.numpy as jnp
from jax import lax
from jax.experimental import pallas as pl
from jax.experimental.pallas import tpu as pltpu
from jax.sharding import PartitionSpec as P

STEPS = 8
LANES = 128
GROUP = 8
LIMIT = 48

flow_rate = 0.02
slide_rate = 0.1
diff_cap = 0.5
time_step = 0.4

unit = (0.25 * flow_rate * 0.5 * time_step) ** (1.0 / 7.0)
slide_unit = 0.5 * time_step * slide_rate / (unit * unit)
cap_unit = 0.5 * time_step * diff_cap


def lanes():
    return lax.broadcasted_iota(jnp.int32, (1, LANES), 1)


def fold(parts):
    parts, bit, lane = list(parts), 1, lanes()
    while bit < len(parts):
        high = (lane & bit) != 0
        for k in range(len(parts)):
            if k & bit == 0:
                x, y = parts[k], parts[k + bit]
                parts[k] = jnp.where(high, pltpu.roll(y, bit, 1), x)
                parts[k + bit] = jnp.where(high, y, pltpu.roll(x, LANES - bit, 1))
        bit *= 2
    return parts


def cut(ref, rows, blocks):
    return [ref[rows, k * LANES : (k + 1) * LANES] for k in range(blocks)]


def fold_all(*refs):
    out = refs[-1]
    blocks, rows = out.shape[1], out.shape[2]

    def tile(r, carry):
        at = pl.ds(pl.multiple_of(r * 8, 8), 8)
        for a, ref in enumerate(refs[:-1]):
            for p, part in enumerate(fold(cut(ref, at, blocks))):
                out[a, p, at, :] = part
        return carry

    lax.fori_loop(0, rows // 8, tile, 0)


def slide_fold(friction, wide, narrow):
    blocks, rows = wide.shape[0], wide.shape[1]
    parts = fold([slide_unit * jnp.exp(-part) for part in cut(friction, slice(0, rows), blocks)])
    for p, part in enumerate(parts):
        wide[p] = part
        narrow[p] = part.astype(narrow.dtype)


def slides(friction):
    rows, columns = friction.shape
    shape = (columns // LANES, rows, LANES)
    return pl.pallas_call(
        slide_fold,
        out_shape=(jax.ShapeDtypeStruct(shape, jnp.float32), jax.ShapeDtypeStruct(shape, jnp.bfloat16)),
        compiler_params=pltpu.CompilerParams(vmem_limit_bytes=8 << 20),
    )(friction)


def direct(strips):
    return min(strips, 4)


def partner(slot, odd):
    other = slot if slot in (0, 3) else 3 - slot
    return other if odd else slot


def pair_at(i, strips, parity):
    together = strips // direct(strips)
    slot = i // together
    if direct(strips) == 4:
        middle = jnp.logical_and(slot > 0, slot < 3)
        slot = jnp.where(jnp.logical_and(middle, parity == 1), 3 - slot, slot)
    return (i % together) * direct(strips) + slot


def weigh(own, coeff_ref, eigen_ref, fields, *refs):
    out, held, given, sems = refs[-5:-4] + refs[-3:] if own else refs
    strips, modes, rows, columns = held.shape
    me = lax.axis_index("modes")
    parity = me % 2 if own else 1 - me % 2

    def copy(p):
        row = (((me // 2) ^ pair_at(p, strips, parity)) * 2 + parity) * rows
        return pltpu.make_async_copy(
            fields.at[:, pl.ds(pl.multiple_of(row, rows), rows), :], held.at[p], sems.at[p]
        )

    small = [
        pltpu.make_async_copy(ref, given.at[i], sems.at[strips + i])
        for i, ref in enumerate((coeff_ref, eigen_ref))
    ]
    for one in small:
        one.start()

    def begin(p, carry):
        copy(p).start()
        return carry

    lax.fori_loop(0, strips, begin, 0)
    if own:
        fold_all(*refs[:-5], refs[-4])
    for one in small:
        one.wait()
    weights = given[0] / jnp.sqrt(1.0 + given[1])
    weights = weights.astype(jnp.bfloat16).astype(jnp.float32)
    at = lax.broadcasted_iota(jnp.int32, weights.shape, 1)
    scale = [
        jnp.sum(jnp.where(at == me * modes + k, weights, 0.0), axis=1, keepdims=True)
        for k in range(modes)
    ]

    def strip(p, carry):
        copy(p).wait()
        for b in range(columns // LANES):
            span = slice(b * LANES, (b + 1) * LANES)
            total = scale[0] * held[p, 0, :, span].astype(jnp.float32)
            for k in range(1, modes):
                total = total + scale[k] * held[p, k, :, span].astype(jnp.float32)
            out[p, :, span] = total.astype(out.dtype)
        return carry

    lax.fori_loop(0, strips, strip, 0)


def shares(coeff, eigen, mode_fields, rows, own, dtype, *statics):
    modes, total_rows, columns = mode_fields.shape
    strips = total_rows // rows // 2

    def kernel(*refs):
        weigh(own, *refs)

    vmem = pl.BlockSpec(memory_space=pltpu.VMEM)
    shapes = [jax.ShapeDtypeStruct((strips, rows, columns), dtype)]
    if own:
        folded = (len(statics), columns // LANES, rows, LANES)
        shapes.append(jax.ShapeDtypeStruct(folded, jnp.float32))
    return pl.pallas_call(
        kernel,
        in_specs=[pl.BlockSpec(memory_space=pltpu.HBM)] * 3 + [vmem] * len(statics),
        out_specs=[vmem] * len(shapes),
        out_shape=shapes,
        scratch_shapes=[
            pltpu.VMEM((strips, modes, rows, columns), jnp.bfloat16),
            pltpu.VMEM((2,) + coeff.shape, jnp.float32),
            pltpu.SemaphoreType.DMA((strips + 2,)),
        ],
        compiler_params=pltpu.CompilerParams(vmem_limit_bytes=LIMIT << 20),
        cost_estimate=pl.CostEstimate(
            flops=modes * total_rows * columns,
            bytes_accessed=modes * total_rows * columns,
            transcendentals=0,
        ),
    )(coeff, eigen, mode_fields, *statics)


PAD = 8
NEVER = -1e30


def wrap(value, to_right, blocks):
    lane = lanes()
    if to_right:
        turned = jnp.where(
            lane >= LANES - blocks,
            pltpu.roll(value, LANES - blocks - 1, 1),
            pltpu.roll(value, LANES - blocks, 1),
        )
        return jnp.where(lane == LANES - 1, 0.0, turned)
    turned = jnp.where(lane < blocks, pltpu.roll(value, blocks + 1, 1), pltpu.roll(value, blocks, 1))
    return jnp.where(lane == 0, 0.0, turned)


def wrap_slots(ref, at, blocks, count):
    for q in range(count):
        ref[blocks + 2 + q, at, :] = wrap(ref[q + 2, at, :], True, blocks)
        ref[1 - q, at, :] = wrap(ref[blocks + 1 - q, at, :], False, blocks)


def spots(rows, reach):
    odd = lax.axis_index("modes") % 2 == 1
    near = pl.multiple_of(PAD + jnp.where(odd, 0, rows + reach), 8)
    far = pl.multiple_of(PAD + jnp.where(odd, rows + reach, 0), 8)
    return pl.ds(PAD + reach, rows), pl.ds(near, reach), pl.ds(far, reach)


def settle(peers, own_s, near_s, far_s, h0, s0, bed, bal, square, steep):
    _, blocks, rows, _ = own_s.shape
    reach = 2 * STEPS
    me = lax.axis_index("modes")
    odd, above, below = me % 2 == 1, me > 0, me < peers - 1
    sides = (None, jnp.where(odd, above, below), jnp.where(odd, below, above))

    def block(p, carry):
        for src, at, inside in zip((own_s, near_s, far_s), spots(rows, reach), sides):
            h, b, m = (src[a, p] for a in range(3))
            h, b, m = unit * h, unit * b, (time_step * unit) * m
            h0[p + 2, at, :] = h
            s0[p + 2, at, :] = h + b
            bed[p + 2, at, :] = b
            bal[p + 2, at, :] = m if inside is None else jnp.where(inside, m, NEVER)
        return carry

    lax.fori_loop(0, blocks, block, 0, unroll=2)
    whole = pl.ds(PAD, rows + 2 * reach)
    wrap_slots(s0, whole, blocks, 2)
    wrap_slots(bed, whole, blocks, 1)
    wrap_slots(h0, whole, blocks, 1)
    zero = jnp.minimum(me, 0)
    up, down = (pl.ds(PAD + off + zero, rows + 2 * reach) for off in (-1, 1))

    def flux(i, carry):
        for q in range((blocks + 2) // 2):
            j = 1 + i * ((blocks + 2) // 2) + q
            gx = s0[j, down, :] - s0[j, up, :]
            gy = s0[j + 1, whole, :] - s0[j - 1, whole, :]
            thick = h0[j, whole, :]
            squared = thick * thick
            square[j, whole, :] = squared
            steep[j, whole, :] = squared * (squared * thick * (gx * gx + gy * gy))
        return carry

    lax.fori_loop(0, 2, flux, 0)


def settled(peers, own_s, near_s, far_s):
    _, blocks, rows, _ = own_s.shape
    shape = (blocks + 4, rows + 4 * STEPS + 2 * PAD, LANES)

    def kernel(*refs):
        settle(peers, *refs)

    return pl.pallas_call(
        kernel,
        out_shape=[jax.ShapeDtypeStruct(shape, jnp.float32)] * 6,
        compiler_params=pltpu.CompilerParams(vmem_limit_bytes=8 << 20),
        cost_estimate=pl.CostEstimate(flops=1, bytes_accessed=1, transcendentals=0),
    )(own_s, near_s, far_s)


def ice(own_f, near_f, far_f, h_in, s_in, bed, bal, square, steep, out, h0, s0, h1, s1, slide, diff):
    blocks, rows, _ = own_f.shape
    reach = 2 * STEPS
    extent = rows + 2 * reach
    zero = jnp.minimum(lax.axis_index("modes"), 0)

    def block(p, carry):
        for src, at in zip((own_f, near_f, far_f), spots(rows, reach)):
            slide[p + 2, at, :] = src[p].astype(jnp.float32)
        return carry

    lax.fori_loop(0, blocks, block, 0, unroll=4)
    wrap_slots(slide, pl.ds(PAD, extent), blocks, 1)

    for step in range(STEPS):
        h, s = (h_in, s_in) if step == 0 else ((h0, s0), (h1, s1))[step % 2]
        hn, sn = ((h1, s1), (h0, s0))[step % 2]
        final = step == STEPS - 1
        edge = 2 * step + 2

        def window(first):
            count = -(-(extent - 2 * first) // 8) * 8
            return [pl.ds(PAD + first + off + zero, count) for off in (-1, 0, 1)]

        up, at, down = window(edge - 1)

        def diffuse(h=h, s=s, at=at, up=up, down=down, step=step):
            for j in range(1, blocks + 3):
                if step == 0:
                    diff[j, at, :] = jnp.minimum(steep[j, at, :] + square[j, at, :] * slide[j, at, :], cap_unit)
                    continue
                gx = s[j, down, :] - s[j, up, :]
                gy = s[j + 1, at, :] - s[j - 1, at, :]
                thick = h[j, at, :]
                squared = thick * thick
                value = squared * (squared * thick * (gx * gx + gy * gy) + slide[j, at, :])
                diff[j, at, :] = jnp.minimum(value, cap_unit)

        diffuse()
        up, at, down = window(edge)

        def flow(i, carry, h=h, s=s, hn=hn, sn=sn, at=at, up=up, down=down, final=final):
            first = 2 + i * count
            s_mid, d_mid = s[first, at, :], diff[first, at, :]
            left = (diff[first - 1, at, :] + d_mid) * (s_mid - s[first - 1, at, :])
            for q in range(count):
                j = first + q
                s_next, d_next = s[j + 1, at, :], diff[j + 1, at, :]
                right = (d_mid + d_next) * (s_next - s_mid)
                total = right - left
                total += (diff[j, down, :] + d_mid) * (s[j, down, :] - s_mid)
                total -= (diff[j, up, :] + d_mid) * (s_mid - s[j, up, :])
                value = jnp.maximum(h[j, at, :] + total + bal[j, at, :], 0.0)
                hn[j, at, :] = value
                if not final:
                    sn[j, at, :] = value + bed[j, at, :]
                left, s_mid, d_mid = right, s_next, d_next
            return carry

        count = min(GROUP, blocks)
        lax.fori_loop(0, blocks // count, flow, 0)
        if not final:
            wrap_slots(sn, at, blocks, 2)
            for slot in (1, blocks + 2):
                hn[slot, at, :] = sn[slot, at, :] - bed[slot, at, :]

    h = h1 if STEPS % 2 else h0

    def tile(r, carry):
        at = pl.ds(pl.multiple_of(r * 8, 8), 8)
        from_at = pl.ds(pl.multiple_of(PAD + reach + r * 8, 8), 8)
        for k, part in enumerate(fold([h[p + 2, from_at, :] * (1.0 / unit) for p in range(blocks)])):
            out[at, k * LANES : (k + 1) * LANES] = part
        return carry

    lax.fori_loop(0, rows // 8, tile, 0, unroll=2)


def march(own_f, near_f, far_f, *state):
    blocks, rows, _ = own_f.shape
    scratch = pltpu.VMEM(state[0].shape, jnp.float32)
    return pl.pallas_call(
        ice,
        out_shape=jax.ShapeDtypeStruct((rows, blocks * LANES), jnp.float32),
        scratch_shapes=[scratch] * 6,
        compiler_params=pltpu.CompilerParams(vmem_limit_bytes=32 << 20),
    )(own_f, near_f, far_f, *state)


def per_device(mode_fields, coeff, eigen, map_friction, bed, smb, thickness):
    peers = lax.axis_size("modes")
    rows, columns = map_friction.shape
    blocks = columns // LANES
    assert rows == 2 * STEPS and peers >= 2 and peers & (peers - 1) == 0
    assert peers >= 4 and columns % LANES == 0 and blocks & (blocks - 1) == 0 and 2 <= blocks <= LANES

    def swap(value, mask):
        return lax.ppermute(value, "modes", [(i, i ^ mask) for i in range(peers)])

    def across(value):
        pairs = [(i, i + 1) for i in range(1, peers - 1, 2)]
        return lax.ppermute(value, "modes", pairs + [(j, i) for i, j in pairs])

    coeff, eigen, mode_fields = (
        pltpu.with_memory_space_constraint(x, pltpu.HBM) for x in (coeff[None], eigen[None], mode_fields)
    )
    (given,) = shares(coeff, eigen, mode_fields, rows, False, jnp.bfloat16)
    kept, statics = shares(coeff, eigen, mode_fields, rows, True, jnp.float32, thickness, bed, smb)
    arrived = swap(given, 1)
    strips = kept.shape[0]
    inner = direct(strips)

    def summed(k):
        at = slice(k * (strips // inner), (k + 1) * (strips // inner))
        return kept[at] + arrived[at].astype(jnp.float32)

    def exchanged(many):
        found = summed(0)[many]
        for k in (1, 2, 3) if inner == 4 else range(1, inner):
            pairs = [(i, i ^ (2 * (partner(k, i % 2) if inner == 4 else k))) for i in range(peers)]
            part = lax.ppermute(summed(k)[many].astype(jnp.float16), "modes", pairs)
            found = found + part.astype(jnp.float32)
        return found

    together = strips // inner
    half = together // 2
    onward = exchanged(slice(half, together)) if half else None
    taken = exchanged(slice(0, max(half, 1)))

    sent = statics.astype(jnp.float16)
    far_s, near_s = across(sent).astype(jnp.float32), swap(sent, 1).astype(jnp.float32)

    onward, sent = lax.optimization_barrier((onward, sent))
    while half:
        taken = taken + swap(onward.astype(jnp.float16), 2 * inner * half).astype(jnp.float32)
        half //= 2
        taken, onward = taken[: max(half, 1)], taken[half:]
    log_friction = map_friction + taken[0]
    sliding, sent = slides(log_friction)
    far_f, near_f = across(sent), swap(sent, 1)
    state = settled(peers, statics, near_s, far_s)
    height = march(sliding, near_f, far_f, *state)
    return (log_friction, height)


def solution(mesh):
    return jax.shard_map(
        per_device,
        mesh=mesh,
        in_specs=(
            P(("groups", "modes"), None, None),
            P("groups"),
            P("groups"),
            P(("groups", "modes"), None),
            P(("groups", "modes"), None),
            P(("groups", "modes"), None),
            P(("groups", "modes"), None),
        ),
        out_specs=(P(("groups", "modes"), None), P(("groups", "modes"), None)),
        check_vma=False,
    )
```

```python
import jax
import jax.numpy as jnp
from jax import lax
from jax.experimental import pallas as pl
from jax.experimental.pallas import tpu as pltpu
from jax.sharding import PartitionSpec as P

STEPS = 8
LANES = 128
GROUP = 8
LIMIT = 48

flow_rate = 0.02
slide_rate = 0.1
diff_cap = 0.5
time_step = 0.4

unit = (0.25 * flow_rate * 0.5 * time_step) ** (1.0 / 7.0)
slide_unit = 0.5 * time_step * slide_rate / (unit * unit)
cap_unit = 0.5 * time_step * diff_cap


def lanes():
    return lax.broadcasted_iota(jnp.int32, (1, LANES), 1)


def fold(parts):
    parts, bit, lane = list(parts), 1, lanes()
    while bit < len(parts):
        high = (lane & bit) != 0
        for k in range(len(parts)):
            if k & bit == 0:
                x, y = parts[k], parts[k + bit]
                parts[k] = jnp.where(high, pltpu.roll(y, bit, 1), x)
                parts[k + bit] = jnp.where(high, y, pltpu.roll(x, LANES - bit, 1))
        bit *= 2
    return parts


def cut(ref, rows, blocks):
    return [ref[rows, k * LANES : (k + 1) * LANES] for k in range(blocks)]


def fold_all(*refs):
    out = refs[-1]
    blocks, rows = out.shape[1], out.shape[2]

    def tile(r, carry):
        at = pl.ds(pl.multiple_of(r * 8, 8), 8)
        for a, ref in enumerate(refs[:-1]):
            for p, part in enumerate(fold(cut(ref, at, blocks))):
                out[a, p, at, :] = part
        return carry

    lax.fori_loop(0, rows // 8, tile, 0)


def slide_fold(friction, wide, narrow):
    blocks, rows = wide.shape[0], wide.shape[1]
    parts = fold([slide_unit * jnp.exp(-part) for part in cut(friction, slice(0, rows), blocks)])
    for p, part in enumerate(parts):
        wide[p] = part
        narrow[p] = part.astype(narrow.dtype)


def slides(friction):
    rows, columns = friction.shape
    shape = (columns // LANES, rows, LANES)
    return pl.pallas_call(
        slide_fold,
        out_shape=(jax.ShapeDtypeStruct(shape, jnp.float32), jax.ShapeDtypeStruct(shape, jnp.bfloat16)),
        compiler_params=pltpu.CompilerParams(vmem_limit_bytes=8 << 20),
    )(friction)


def direct(strips):
    return min(strips, 4)


def partner(slot, odd):
    other = slot if slot in (0, 3) else 3 - slot
    return other if odd else slot


def pair_at(i, strips, parity):
    together = strips // direct(strips)
    slot = i // together
    if direct(strips) == 4:
        middle = jnp.logical_and(slot > 0, slot < 3)
        slot = jnp.where(jnp.logical_and(middle, parity == 1), 3 - slot, slot)
    return (i % together) * direct(strips) + slot


def weigh(own, coeff_ref, eigen_ref, fields, *refs):
    if own:
        early, *others, out, folded, held, given, sems = refs
    else:
        out, early, held, given, sems = refs
    strips, modes, rows, columns = held.shape
    me = lax.axis_index("modes")
    parity = me % 2 if own else 1 - me % 2

    def rows_of(p, parity):
        row = (((me // 2) ^ pair_at(p, strips, parity)) * 2 + parity) * rows
        return fields.at[:, pl.ds(pl.multiple_of(row, rows), rows), :]

    def copy(p):
        return pltpu.make_async_copy(rows_of(p, parity), held.at[p], sems.at[p])

    small = [
        pltpu.make_async_copy(ref, given.at[i], sems.at[strips + i])
        for i, ref in enumerate((coeff_ref, eigen_ref))
    ]
    for one in small:
        one.start()

    def begin(p, carry):
        copy(p).start()
        return carry

    lax.fori_loop(1 if own else 0, strips, begin, 0)
    if own:
        fold_all(*others, folded)
    else:
        ahead = pltpu.make_async_copy(rows_of(0, me % 2), early, sems.at[strips + 2])
        ahead.start()
    for one in small:
        one.wait()
    weights = given[0] / jnp.sqrt(1.0 + given[1])
    weights = weights.astype(jnp.bfloat16).astype(jnp.float32)
    at = lax.broadcasted_iota(jnp.int32, weights.shape, 1)
    scale = [
        jnp.sum(jnp.where(at == me * modes + k, weights, 0.0), axis=1, keepdims=True)
        for k in range(modes)
    ]

    def sums(p, source):
        for b in range(columns // LANES):
            span = slice(b * LANES, (b + 1) * LANES)
            total = scale[0] * source[0, :, span].astype(jnp.float32)
            for k in range(1, modes):
                total = total + scale[k] * source[k, :, span].astype(jnp.float32)
            out[p, :, span] = total.astype(out.dtype)

    def strip(p, carry):
        copy(p).wait()
        sums(p, held.at[p])
        return carry

    if own:
        sums(0, early)
    lax.fori_loop(1 if own else 0, strips, strip, 0)
    if not own:
        ahead.wait()


def shares(coeff, eigen, mode_fields, rows, own, dtype, *statics):
    modes, total_rows, columns = mode_fields.shape
    strips = total_rows // rows // 2

    def kernel(*refs):
        weigh(own, *refs)

    vmem = pl.BlockSpec(memory_space=pltpu.VMEM)
    shapes = [jax.ShapeDtypeStruct((strips, rows, columns), dtype)]
    if own:
        folded = (len(statics) - 1, columns // LANES, rows, LANES)
        shapes.append(jax.ShapeDtypeStruct(folded, jnp.float32))
    else:
        shapes.append(jax.ShapeDtypeStruct((modes, rows, columns), jnp.bfloat16))
    return pl.pallas_call(
        kernel,
        in_specs=[pl.BlockSpec(memory_space=pltpu.HBM)] * 3 + [vmem] * len(statics),
        out_specs=[vmem] * len(shapes),
        out_shape=shapes,
        scratch_shapes=[
            pltpu.VMEM((strips, modes, rows, columns), jnp.bfloat16),
            pltpu.VMEM((2,) + coeff.shape, jnp.float32),
            pltpu.SemaphoreType.DMA((strips + 3,)),
        ],
        compiler_params=pltpu.CompilerParams(vmem_limit_bytes=LIMIT << 20),
        cost_estimate=pl.CostEstimate(
            flops=modes * total_rows * columns,
            bytes_accessed=modes * total_rows * columns,
            transcendentals=0,
        ),
    )(coeff, eigen, mode_fields, *statics)


PAD = 8
NEVER = -1e30


def wrap(value, to_right, blocks):
    lane = lanes()
    if to_right:
        turned = jnp.where(
            lane >= LANES - blocks,
            pltpu.roll(value, LANES - blocks - 1, 1),
            pltpu.roll(value, LANES - blocks, 1),
        )
        return jnp.where(lane == LANES - 1, 0.0, turned)
    turned = jnp.where(lane < blocks, pltpu.roll(value, blocks + 1, 1), pltpu.roll(value, blocks, 1))
    return jnp.where(lane == 0, 0.0, turned)


def wrap_slots(ref, at, blocks, count):
    for q in range(count):
        ref[blocks + 2 + q, at, :] = wrap(ref[q + 2, at, :], True, blocks)
        ref[1 - q, at, :] = wrap(ref[blocks + 1 - q, at, :], False, blocks)


def spots(rows, reach):
    odd = lax.axis_index("modes") % 2 == 1
    near = pl.multiple_of(PAD + jnp.where(odd, 0, rows + reach), 8)
    far = pl.multiple_of(PAD + jnp.where(odd, rows + reach, 0), 8)
    return pl.ds(PAD + reach, rows), pl.ds(near, reach), pl.ds(far, reach)


def settle(peers, own_s, near_s, far_s, h0, s0, bed, bal, square, steep):
    _, blocks, rows, _ = own_s.shape
    reach = 2 * STEPS
    me = lax.axis_index("modes")
    odd, above, below = me % 2 == 1, me > 0, me < peers - 1
    sides = (None, jnp.where(odd, above, below), jnp.where(odd, below, above))

    def block(p, carry):
        for src, at, inside in zip((own_s, near_s, far_s), spots(rows, reach), sides):
            h, b, m = (src[a, p] for a in range(3))
            h, b, m = unit * h, unit * b, (time_step * unit) * m
            h0[p + 2, at, :] = h
            s0[p + 2, at, :] = h + b
            bed[p + 2, at, :] = b
            bal[p + 2, at, :] = m if inside is None else jnp.where(inside, m, NEVER)
        return carry

    lax.fori_loop(0, blocks, block, 0, unroll=2)
    whole = pl.ds(PAD, rows + 2 * reach)
    wrap_slots(s0, whole, blocks, 2)
    wrap_slots(bed, whole, blocks, 1)
    wrap_slots(h0, whole, blocks, 1)
    zero = jnp.minimum(me, 0)
    up, down = (pl.ds(PAD + off + zero, rows + 2 * reach) for off in (-1, 1))

    def flux(i, carry):
        for q in range((blocks + 2) // 2):
            j = 1 + i * ((blocks + 2) // 2) + q
            gx = s0[j, down, :] - s0[j, up, :]
            gy = s0[j + 1, whole, :] - s0[j - 1, whole, :]
            thick = h0[j, whole, :]
            squared = thick * thick
            square[j, whole, :] = squared
            steep[j, whole, :] = squared * (squared * thick * (gx * gx + gy * gy))
        return carry

    lax.fori_loop(0, 2, flux, 0)


def settled(peers, own_s, near_s, far_s):
    _, blocks, rows, _ = own_s.shape
    shape = (blocks + 4, rows + 4 * STEPS + 2 * PAD, LANES)

    def kernel(*refs):
        settle(peers, *refs)

    return pl.pallas_call(
        kernel,
        out_shape=[jax.ShapeDtypeStruct(shape, jnp.float32)] * 6,
        compiler_params=pltpu.CompilerParams(vmem_limit_bytes=8 << 20),
        cost_estimate=pl.CostEstimate(flops=1, bytes_accessed=1, transcendentals=0),
    )(own_s, near_s, far_s)


def ice(own_f, near_f, far_f, h_in, s_in, bed, bal, square, steep, out, h0, s0, h1, s1, slide, diff):
    blocks, rows, _ = own_f.shape
    reach = 2 * STEPS
    extent = rows + 2 * reach
    zero = jnp.minimum(lax.axis_index("modes"), 0)

    def block(p, carry):
        for src, at in zip((own_f, near_f, far_f), spots(rows, reach)):
            slide[p + 2, at, :] = src[p].astype(jnp.float32)
        return carry

    lax.fori_loop(0, blocks, block, 0, unroll=4)
    wrap_slots(slide, pl.ds(PAD, extent), blocks, 1)

    for step in range(STEPS):
        h, s = (h_in, s_in) if step == 0 else ((h0, s0), (h1, s1))[step % 2]
        hn, sn = ((h1, s1), (h0, s0))[step % 2]
        final = step == STEPS - 1
        edge = 2 * step + 2

        def window(first):
            count = -(-(extent - 2 * first) // 8) * 8
            return [pl.ds(PAD + first + off + zero, count) for off in (-1, 0, 1)]

        up, at, down = window(edge - 1)

        def diffuse(h=h, s=s, at=at, up=up, down=down, step=step):
            for j in range(1, blocks + 3):
                if step == 0:
                    diff[j, at, :] = jnp.minimum(steep[j, at, :] + square[j, at, :] * slide[j, at, :], cap_unit)
                    continue
                gx = s[j, down, :] - s[j, up, :]
                gy = s[j + 1, at, :] - s[j - 1, at, :]
                thick = h[j, at, :]
                squared = thick * thick
                value = squared * (squared * thick * (gx * gx + gy * gy) + slide[j, at, :])
                diff[j, at, :] = jnp.minimum(value, cap_unit)

        diffuse()
        up, at, down = window(edge)

        def flow(i, carry, h=h, s=s, hn=hn, sn=sn, at=at, up=up, down=down, final=final):
            first = 2 + i * count
            s_mid, d_mid = s[first, at, :], diff[first, at, :]
            left = (diff[first - 1, at, :] + d_mid) * (s_mid - s[first - 1, at, :])
            for q in range(count):
                j = first + q
                s_next, d_next = s[j + 1, at, :], diff[j + 1, at, :]
                right = (d_mid + d_next) * (s_next - s_mid)
                total = right - left
                total += (diff[j, down, :] + d_mid) * (s[j, down, :] - s_mid)
                total -= (diff[j, up, :] + d_mid) * (s_mid - s[j, up, :])
                value = jnp.maximum(h[j, at, :] + total + bal[j, at, :], 0.0)
                hn[j, at, :] = value
                if not final:
                    sn[j, at, :] = value + bed[j, at, :]
                left, s_mid, d_mid = right, s_next, d_next
            return carry

        count = min(GROUP, blocks)
        lax.fori_loop(0, blocks // count, flow, 0)
        if not final:
            wrap_slots(sn, at, blocks, 2)
            for slot in (1, blocks + 2):
                hn[slot, at, :] = sn[slot, at, :] - bed[slot, at, :]

    h = h1 if STEPS % 2 else h0

    def tile(r, carry):
        at = pl.ds(pl.multiple_of(r * 8, 8), 8)
        from_at = pl.ds(pl.multiple_of(PAD + reach + r * 8, 8), 8)
        for k, part in enumerate(fold([h[p + 2, from_at, :] * (1.0 / unit) for p in range(blocks)])):
            out[at, k * LANES : (k + 1) * LANES] = part
        return carry

    lax.fori_loop(0, rows // 8, tile, 0, unroll=2)


def march(own_f, near_f, far_f, *state):
    blocks, rows, _ = own_f.shape
    scratch = pltpu.VMEM(state[0].shape, jnp.float32)
    return pl.pallas_call(
        ice,
        out_shape=jax.ShapeDtypeStruct((rows, blocks * LANES), jnp.float32),
        scratch_shapes=[scratch] * 6,
        compiler_params=pltpu.CompilerParams(vmem_limit_bytes=32 << 20),
    )(own_f, near_f, far_f, *state)


def per_device(mode_fields, coeff, eigen, map_friction, bed, smb, thickness):
    peers = lax.axis_size("modes")
    rows, columns = map_friction.shape
    blocks = columns // LANES
    assert rows == 2 * STEPS and peers >= 2 and peers & (peers - 1) == 0
    assert peers >= 4 and columns % LANES == 0 and blocks & (blocks - 1) == 0 and 2 <= blocks <= LANES

    def swap(value, mask):
        return lax.ppermute(value, "modes", [(i, i ^ mask) for i in range(peers)])

    def across(value):
        pairs = [(i, i + 1) for i in range(1, peers - 1, 2)]
        return lax.ppermute(value, "modes", pairs + [(j, i) for i, j in pairs])

    coeff, eigen, mode_fields = (
        pltpu.with_memory_space_constraint(x, pltpu.HBM) for x in (coeff[None], eigen[None], mode_fields)
    )
    given, early = shares(coeff, eigen, mode_fields, rows, False, jnp.bfloat16)
    kept, statics = shares(coeff, eigen, mode_fields, rows, True, jnp.float32, early, thickness, bed, smb)
    arrived = swap(given, 1)
    strips = kept.shape[0]
    inner = direct(strips)

    def summed(k):
        at = slice(k * (strips // inner), (k + 1) * (strips // inner))
        return kept[at] + arrived[at].astype(jnp.float32)

    def exchanged(many):
        found = summed(0)[many]
        for k in (1, 2, 3) if inner == 4 else range(1, inner):
            pairs = [(i, i ^ (2 * (partner(k, i % 2) if inner == 4 else k))) for i in range(peers)]
            part = lax.ppermute(summed(k)[many].astype(jnp.float16), "modes", pairs)
            found = found + part.astype(jnp.float32)
        return found

    together = strips // inner
    half = together // 2
    onward = exchanged(slice(half, together)) if half else None
    taken = exchanged(slice(0, max(half, 1)))

    sent = statics.astype(jnp.float16)
    far_s, near_s = across(sent).astype(jnp.float32), swap(sent, 1).astype(jnp.float32)

    onward, sent = lax.optimization_barrier((onward, sent))
    while half:
        taken = taken + swap(onward.astype(jnp.float16), 2 * inner * half).astype(jnp.float32)
        half //= 2
        taken, onward = taken[: max(half, 1)], taken[half:]
    log_friction = map_friction + taken[0]
    sliding, sent = slides(log_friction)
    far_f, near_f = across(sent), swap(sent, 1)
    state = settled(peers, statics, near_s, far_s)
    height = march(sliding, near_f, far_f, *state)
    return (log_friction, height)


def solution(mesh):
    return jax.shard_map(
        per_device,
        mesh=mesh,
        in_specs=(
            P(("groups", "modes"), None, None),
            P("groups"),
            P("groups"),
            P(("groups", "modes"), None),
            P(("groups", "modes"), None),
            P(("groups", "modes"), None),
            P(("groups", "modes"), None),
        ),
        out_specs=(P(("groups", "modes"), None), P(("groups", "modes"), None)),
        check_vma=False,
    )
```

```python
import jax
import jax.numpy as jnp
from jax import lax
from jax.experimental import pallas as pl
from jax.experimental.pallas import tpu as pltpu
from jax.sharding import PartitionSpec as P

STEPS = 8
LANES = 128
GROUP = 8
LIMIT = 48

flow_rate = 0.02
slide_rate = 0.1
diff_cap = 0.5
time_step = 0.4

unit = (0.25 * flow_rate * 0.5 * time_step) ** (1.0 / 7.0)
slide_unit = 0.5 * time_step * slide_rate / (unit * unit)
cap_unit = 0.5 * time_step * diff_cap


def lanes():
    return lax.broadcasted_iota(jnp.int32, (1, LANES), 1)


def fold(parts):
    parts, bit, lane = list(parts), 1, lanes()
    while bit < len(parts):
        high = (lane & bit) != 0
        for k in range(len(parts)):
            if k & bit == 0:
                x, y = parts[k], parts[k + bit]
                parts[k] = jnp.where(high, pltpu.roll(y, bit, 1), x)
                parts[k + bit] = jnp.where(high, y, pltpu.roll(x, LANES - bit, 1))
        bit *= 2
    return parts


def cut(ref, rows, blocks):
    return [ref[rows, k * LANES : (k + 1) * LANES] for k in range(blocks)]


def fold_all(*refs):
    out = refs[-1]
    blocks, rows = out.shape[1], out.shape[2]

    def tile(r, carry):
        at = pl.ds(pl.multiple_of(r * 8, 8), 8)
        for a, ref in enumerate(refs[:-1]):
            for p, part in enumerate(fold(cut(ref, at, blocks))):
                out[a, p, at, :] = part
        return carry

    lax.fori_loop(0, rows // 8, tile, 0)


def slide_fold(friction, wide, narrow):
    blocks, rows = wide.shape[0], wide.shape[1]
    parts = fold([slide_unit * jnp.exp(-part) for part in cut(friction, slice(0, rows), blocks)])
    for p, part in enumerate(parts):
        wide[p] = part
        narrow[p] = part.astype(narrow.dtype)


def slides(friction):
    rows, columns = friction.shape
    shape = (columns // LANES, rows, LANES)
    return pl.pallas_call(
        slide_fold,
        out_shape=(jax.ShapeDtypeStruct(shape, jnp.float32), jax.ShapeDtypeStruct(shape, jnp.bfloat16)),
        compiler_params=pltpu.CompilerParams(vmem_limit_bytes=8 << 20),
    )(friction)


def direct(strips):
    return min(strips, 4)


def partner(slot, odd):
    other = slot if slot in (0, 3) else 3 - slot
    return other if odd else slot


def pair_at(i, strips, parity):
    together = strips // direct(strips)
    slot = i // together
    if direct(strips) == 4:
        middle = jnp.logical_and(slot > 0, slot < 3)
        slot = jnp.where(jnp.logical_and(middle, parity == 1), 3 - slot, slot)
    return (i % together) * direct(strips) + slot


def weigh(own, coeff_ref, eigen_ref, fields, *refs):
    if own:
        early, *others, out, folded, held, given, sems = refs
    else:
        out, early, held, given, sems = refs
    strips, modes, rows, columns = held.shape
    me = lax.axis_index("modes")
    parity = me % 2 if own else 1 - me % 2

    def rows_of(p, parity):
        row = (((me // 2) ^ pair_at(p, strips, parity)) * 2 + parity) * rows
        return fields.at[:, pl.ds(pl.multiple_of(row, rows), rows), :]

    def copy(p):
        return pltpu.make_async_copy(rows_of(p, parity), held.at[p], sems.at[p])

    small = [
        pltpu.make_async_copy(ref, given.at[i], sems.at[strips + i])
        for i, ref in enumerate((coeff_ref, eigen_ref))
    ]
    for one in small:
        one.start()

    def begin(p, carry):
        copy(p).start()
        return carry

    lax.fori_loop(1 if own else 0, strips, begin, 0)
    if own:
        fold_all(*others, folded)
    else:
        ahead = pltpu.make_async_copy(rows_of(0, me % 2), early, sems.at[strips + 2])
        ahead.start()
    for one in small:
        one.wait()
    weights = given[0] / jnp.sqrt(1.0 + given[1])
    weights = weights.astype(jnp.bfloat16).astype(jnp.float32)
    at = lax.broadcasted_iota(jnp.int32, weights.shape, 1)
    scale = [
        jnp.sum(jnp.where(at == me * modes + k, weights, 0.0), axis=1, keepdims=True)
        for k in range(modes)
    ]

    def sums(p, source):
        for b in range(columns // LANES):
            span = slice(b * LANES, (b + 1) * LANES)
            total = scale[0] * source[0, :, span].astype(jnp.float32)
            for k in range(1, modes):
                total = total + scale[k] * source[k, :, span].astype(jnp.float32)
            out[p, :, span] = total.astype(out.dtype)

    def strip(p, carry):
        copy(p).wait()
        sums(p, held.at[p])
        return carry

    if own:
        sums(0, early)
    lax.fori_loop(1 if own else 0, strips, strip, 0)
    if not own:
        ahead.wait()


def shares(coeff, eigen, mode_fields, rows, own, dtype, *statics):
    modes, total_rows, columns = mode_fields.shape
    strips = total_rows // rows // 2

    def kernel(*refs):
        weigh(own, *refs)

    vmem = pl.BlockSpec(memory_space=pltpu.VMEM)
    shapes = [jax.ShapeDtypeStruct((strips, rows, columns), dtype)]
    if own:
        folded = (len(statics) - 1, columns // LANES, rows, LANES)
        shapes.append(jax.ShapeDtypeStruct(folded, jnp.float32))
    else:
        shapes.append(jax.ShapeDtypeStruct((modes, rows, columns), jnp.bfloat16))
    return pl.pallas_call(
        kernel,
        in_specs=[pl.BlockSpec(memory_space=pltpu.HBM)] * 3 + [vmem] * len(statics),
        out_specs=[vmem] * len(shapes),
        out_shape=shapes,
        scratch_shapes=[
            pltpu.VMEM((strips, modes, rows, columns), jnp.bfloat16),
            pltpu.VMEM((2,) + coeff.shape, jnp.float32),
            pltpu.SemaphoreType.DMA((strips + 3,)),
        ],
        compiler_params=pltpu.CompilerParams(vmem_limit_bytes=LIMIT << 20),
        cost_estimate=pl.CostEstimate(
            flops=modes * total_rows * columns,
            bytes_accessed=modes * total_rows * columns,
            transcendentals=0,
        ),
    )(coeff, eigen, mode_fields, *statics)


PAD = 8
NEVER = -1e30


def wrap(value, to_right, blocks):
    lane = lanes()
    if to_right:
        turned = jnp.where(
            lane >= LANES - blocks,
            pltpu.roll(value, LANES - blocks - 1, 1),
            pltpu.roll(value, LANES - blocks, 1),
        )
        return jnp.where(lane == LANES - 1, 0.0, turned)
    turned = jnp.where(lane < blocks, pltpu.roll(value, blocks + 1, 1), pltpu.roll(value, blocks, 1))
    return jnp.where(lane == 0, 0.0, turned)


def wrap_slots(ref, at, blocks, count):
    for q in range(count):
        ref[blocks + 2 + q, at, :] = wrap(ref[q + 2, at, :], True, blocks)
        ref[1 - q, at, :] = wrap(ref[blocks + 1 - q, at, :], False, blocks)


def spots(rows, reach):
    odd = lax.axis_index("modes") % 2 == 1
    near = pl.multiple_of(PAD + jnp.where(odd, 0, rows + reach), 8)
    far = pl.multiple_of(PAD + jnp.where(odd, rows + reach, 0), 8)
    return pl.ds(PAD + reach, rows), pl.ds(near, reach), pl.ds(far, reach)


def settle(peers, own_s, near_s, far_s, h0, s0, bed, bal, square, steep):
    _, blocks, rows, _ = own_s.shape
    reach = 2 * STEPS
    me = lax.axis_index("modes")
    odd, above, below = me % 2 == 1, me > 0, me < peers - 1
    sides = (None, jnp.where(odd, above, below), jnp.where(odd, below, above))

    def block(p, carry):
        for src, at, inside in zip((own_s, near_s, far_s), spots(rows, reach), sides):
            h, b, m = (src[a, p] for a in range(3))
            h, b, m = unit * h, unit * b, (time_step * unit) * m
            h0[p + 2, at, :] = h
            s0[p + 2, at, :] = h + b
            bed[p + 2, at, :] = b
            bal[p + 2, at, :] = m if inside is None else jnp.where(inside, m, NEVER)
        return carry

    lax.fori_loop(0, blocks, block, 0, unroll=2)
    whole = pl.ds(PAD, rows + 2 * reach)
    wrap_slots(s0, whole, blocks, 2)
    wrap_slots(bed, whole, blocks, 1)
    wrap_slots(h0, whole, blocks, 1)
    zero = jnp.minimum(me, 0)
    up, down = (pl.ds(PAD + off + zero, rows + 2 * reach) for off in (-1, 1))

    def flux(i, carry):
        for q in range((blocks + 2) // 2):
            j = 1 + i * ((blocks + 2) // 2) + q
            gx = s0[j, down, :] - s0[j, up, :]
            gy = s0[j + 1, whole, :] - s0[j - 1, whole, :]
            thick = h0[j, whole, :]
            squared = thick * thick
            square[j, whole, :] = squared
            steep[j, whole, :] = squared * (squared * thick * (gx * gx + gy * gy))
        return carry

    lax.fori_loop(0, 2, flux, 0)


def settled(peers, own_s, near_s, far_s):
    _, blocks, rows, _ = own_s.shape
    shape = (blocks + 4, rows + 4 * STEPS + 2 * PAD, LANES)

    def kernel(*refs):
        settle(peers, *refs)

    return pl.pallas_call(
        kernel,
        out_shape=[jax.ShapeDtypeStruct(shape, jnp.float32)] * 6,
        compiler_params=pltpu.CompilerParams(vmem_limit_bytes=8 << 20),
        cost_estimate=pl.CostEstimate(flops=1, bytes_accessed=1, transcendentals=0),
    )(own_s, near_s, far_s)


def ice(own_f, near_f, far_f, h_in, s_in, bed, bal, square, steep, out, h0, s0, h1, s1, slide, diff):
    blocks, rows, _ = own_f.shape
    reach = 2 * STEPS
    extent = rows + 2 * reach
    zero = jnp.minimum(lax.axis_index("modes"), 0)

    def block(p, carry):
        for src, at in zip((own_f, near_f, far_f), spots(rows, reach)):
            slide[p + 2, at, :] = src[p].astype(jnp.float32)
        return carry

    lax.fori_loop(0, blocks, block, 0, unroll=4)
    wrap_slots(slide, pl.ds(PAD, extent), blocks, 1)

    for step in range(STEPS):
        h, s = (h_in, s_in) if step == 0 else ((h0, s0), (h1, s1))[step % 2]
        hn, sn = ((h1, s1), (h0, s0))[step % 2]
        final = step == STEPS - 1
        edge = 2 * step + 2

        def window(first):
            count = -(-(extent - 2 * first) // 8) * 8
            return [pl.ds(PAD + first + off + zero, count) for off in (-1, 0, 1)]

        up, at, down = window(edge - 1)

        def diffuse(h=h, s=s, at=at, up=up, down=down, step=step):
            for j in range(1, blocks + 3):
                if step == 0:
                    diff[j, at, :] = jnp.minimum(steep[j, at, :] + square[j, at, :] * slide[j, at, :], cap_unit)
                    continue
                gx = s[j, down, :] - s[j, up, :]
                gy = s[j + 1, at, :] - s[j - 1, at, :]
                thick = h[j, at, :]
                squared = thick * thick
                value = squared * (squared * thick * (gx * gx + gy * gy) + slide[j, at, :])
                diff[j, at, :] = jnp.minimum(value, cap_unit)

        diffuse()
        up, at, down = window(edge)

        def flow(i, carry, h=h, s=s, hn=hn, sn=sn, at=at, up=up, down=down, final=final):
            first = 2 + i * count
            s_mid, d_mid = s[first, at, :], diff[first, at, :]
            left = (diff[first - 1, at, :] + d_mid) * (s_mid - s[first - 1, at, :])
            for q in range(count):
                j = first + q
                s_next, d_next = s[j + 1, at, :], diff[j + 1, at, :]
                right = (d_mid + d_next) * (s_next - s_mid)
                total = right - left
                total += (diff[j, down, :] + d_mid) * (s[j, down, :] - s_mid)
                total -= (diff[j, up, :] + d_mid) * (s_mid - s[j, up, :])
                value = jnp.maximum(h[j, at, :] + total + bal[j, at, :], 0.0)
                hn[j, at, :] = value
                if not final:
                    sn[j, at, :] = value + bed[j, at, :]
                left, s_mid, d_mid = right, s_next, d_next
            return carry

        count = min(GROUP, blocks)
        lax.fori_loop(0, blocks // count, flow, 0)
        if not final:
            wrap_slots(sn, at, blocks, 2)
            for slot in (1, blocks + 2):
                hn[slot, at, :] = sn[slot, at, :] - bed[slot, at, :]

    h = h1 if STEPS % 2 else h0

    def tile(r, carry):
        at = pl.ds(pl.multiple_of(r * 8, 8), 8)
        from_at = pl.ds(pl.multiple_of(PAD + reach + r * 8, 8), 8)
        for k, part in enumerate(fold([h[p + 2, from_at, :] * (1.0 / unit) for p in range(blocks)])):
            out[at, k * LANES : (k + 1) * LANES] = part
        return carry

    lax.fori_loop(0, rows // 8, tile, 0, unroll=2)


def march(own_f, near_f, far_f, *state):
    blocks, rows, _ = own_f.shape
    scratch = pltpu.VMEM(state[0].shape, jnp.float32)
    return pl.pallas_call(
        ice,
        out_shape=jax.ShapeDtypeStruct((rows, blocks * LANES), jnp.float32),
        scratch_shapes=[scratch] * 6,
        compiler_params=pltpu.CompilerParams(vmem_limit_bytes=32 << 20),
    )(own_f, near_f, far_f, *state)


def per_device(mode_fields, coeff, eigen, map_friction, bed, smb, thickness):
    peers = lax.axis_size("modes")
    rows, columns = map_friction.shape
    blocks = columns // LANES
    assert rows == 2 * STEPS and peers >= 2 and peers & (peers - 1) == 0
    assert peers >= 4 and columns % LANES == 0 and blocks & (blocks - 1) == 0 and 2 <= blocks <= LANES

    def swap(value, mask):
        return lax.ppermute(value, "modes", [(i, i ^ mask) for i in range(peers)])

    def across(value):
        pairs = [(i, i + 1) for i in range(1, peers - 1, 2)]
        return lax.ppermute(value, "modes", pairs + [(j, i) for i, j in pairs])

    coeff, eigen, mode_fields = (
        pltpu.with_memory_space_constraint(x, pltpu.HBM) for x in (coeff[None], eigen[None], mode_fields)
    )
    given, early = shares(coeff, eigen, mode_fields, rows, False, jnp.bfloat16)
    kept, statics = shares(coeff, eigen, mode_fields, rows, True, jnp.float32, early, thickness, bed, smb)
    arrived = swap(given, 1)
    strips = kept.shape[0]
    inner = direct(strips)

    def summed(k):
        at = slice(k * (strips // inner), (k + 1) * (strips // inner))
        return kept[at] + arrived[at].astype(jnp.float32)

    def exchanged(many):
        found = summed(0)[many]
        for k in (1, 2, 3) if inner == 4 else range(1, inner):
            pairs = [(i, i ^ (2 * (partner(k, i % 2) if inner == 4 else k))) for i in range(peers)]
            part = lax.ppermute(summed(k)[many].astype(jnp.float16), "modes", pairs)
            found = found + part.astype(jnp.float32)
        return found

    together = strips // inner
    half = together // 2
    onward = exchanged(slice(half, together)) if half else None
    taken = exchanged(slice(0, max(half, 1)))

    sent = statics.astype(jnp.float16)
    near_s, far_s = swap(sent, 1).astype(jnp.float32), across(sent).astype(jnp.float32)

    onward, sent = lax.optimization_barrier((onward, sent))
    while half:
        taken = taken + swap(onward.astype(jnp.float16), 2 * inner * half).astype(jnp.float32)
        half //= 2
        taken, onward = taken[: max(half, 1)], taken[half:]
    log_friction = map_friction + taken[0]
    sliding, sent = slides(log_friction)
    far_f, near_f = across(sent), swap(sent, 1)
    state = settled(peers, statics, near_s, far_s)
    height = march(sliding, near_f, far_f, *state)
    return (log_friction, height)


def solution(mesh):
    return jax.shard_map(
        per_device,
        mesh=mesh,
        in_specs=(
            P(("groups", "modes"), None, None),
            P("groups"),
            P("groups"),
            P(("groups", "modes"), None),
            P(("groups", "modes"), None),
            P(("groups", "modes"), None),
            P(("groups", "modes"), None),
        ),
        out_specs=(P(("groups", "modes"), None), P(("groups", "modes"), None)),
        check_vma=False,
    )
```
